256 devices in a mesh: sub: 16 (over z, core), row: 16 (over y, x).
Axes of the slice: x: 4, y: 4, z: 8, core: 2. Of those that a mesh axis runs over, the one named last changes fastest.
Arguments:
- modes: float32 [196608, 64], P(('sub', 'row')), may hold values from -6 to 6
- search: float32 [196608, 64], P(('sub', 'row')), may hold values from -6 to 6
- precond: float32 [196608], P(('sub', 'row')), may hold values from 0.05 to 0.25
- in_row: int32 [16, 16, 96], P('sub', 'row'), may hold values from 0 to 11, as said below
- in_col: int32 [16, 16, 96], P('sub', 'row'), may hold values from 0 to 191, as said below
- in_val: bfloat16 [16, 16, 96, 64, 64], P('sub', 'row'), as said below
- bnd_rows: int32 [16, 16, 3], P('sub', 'row'), may hold values from 0 to 11, as said below
- if_row: int32 [16, 16, 12], P('sub', 'row'), may hold values from 0 to 11, as said below
- if_src: int32 [16, 16, 12], P('sub', 'row'), may hold values from 0 to 47, as said below
- if_val: bfloat16 [16, 16, 12, 64, 64], P('sub', 'row')
Outputs:
- modes_out: float32 [196608, 64], P(('sub', 'row'))
- search_out: float32 [196608, 64], P(('sub', 'row'))
The draws below stay inside these ranges and needn't reach their ends.
Inputs may be any that keep to these rules, and one draw needn't show every extreme that they name: `in_row`: entry k < 12 is k; each later group of 12 entries names each of the device's block-rows once. `in_col`: entry k < 12 is r * 12 + k on device (s, r); in each later group of 12 entries the devices of a subdomain together name each of its 192 block-rows once, and no entry names its own block-row. `in_val`: the first 12 blocks of every device are symmetric; the operator A is symmetric positive definite. `bnd_rows`: distinct within a device. `if_row`: each of the device's 12 block-rows once. `if_src`: t * 3 + q with t never the device's own subdomain; among the devices with one index of row, each boundary slot of each subdomain is named exactly 4 times.
All inputs are finite; a program needn't handle non-finite values.
Results may differ from the reference program's by a relative error of at most 0.0006.
Values may be sent and summed in bfloat16 or wider, within the bound.
A program may use at most 128 MiB of HBM per device.

```python
import math
import jax
import jax.numpy as jnp
from jax import lax

NMODE = 64
KB = 64
LB = 12
ITERS = 2
NIN = 96
IFR = 3
NIF = 12
SUBB = 192
ROWS = 196608
N_SUB = 16
N_ROW = 16


def intra_pattern(key):
    base = jax.random.fold_in(key, 11)
    first_key, second_key = jax.random.split(base)
    groups = NIN // LB - 1
    ladder = jnp.broadcast_to(jnp.arange(LB, dtype=jnp.int32), (N_SUB, N_ROW, groups, LB))
    rows_extra = jax.random.permutation(first_key, ladder, axis=-1, independent=True).astype(jnp.int32)
    shifts = jax.random.randint(second_key, (N_SUB, 1, groups, 1), 1, SUBB).astype(jnp.int32)
    owner = jnp.arange(N_ROW, dtype=jnp.int32)[None, :, None, None] * LB
    cols_extra = ((owner + rows_extra + shifts) % SUBB).astype(jnp.int32)
    diagonal_rows = jnp.broadcast_to(jnp.arange(LB, dtype=jnp.int32)[None, None, :], (N_SUB, N_ROW, LB))
    rows_all = jnp.concatenate([diagonal_rows, rows_extra.reshape(N_SUB, N_ROW, groups * LB)], -1)
    cols_all = jnp.concatenate([owner[..., 0] + diagonal_rows, cols_extra.reshape(N_SUB, N_ROW, groups * LB)], -1)
    return (rows_all.astype(jnp.int32), cols_all.astype(jnp.int32))


def draw_in_row(key, part):
    return intra_pattern(key)[0]


def draw_in_col(key, part):
    return intra_pattern(key)[1]


def draw_in_val(key, part):
    base = jax.random.fold_in(key, 23)
    first_key, second_key, third_key = jax.random.split(base, 3)
    spread = 0.5 / KB
    raw = jax.random.uniform(first_key, (N_SUB, N_ROW, NIN, KB, KB), jnp.float32, -spread, spread)
    level = jax.random.uniform(second_key, (N_SUB, N_ROW, NIN, KB), jnp.float32, 2.0, 6.0)
    coupling = jnp.exp(jax.random.uniform(third_key, (N_SUB, N_ROW, NIN, 1, 1), jnp.float32, math.log(0.25), math.log(1.0)))
    identity = (jnp.arange(KB)[:, None] == jnp.arange(KB)[None, :]).astype(jnp.float32)
    symmetric = 0.5 * (raw + jnp.swapaxes(raw, -1, -2)) + identity * (36.0 + level[..., None])
    off_block = raw - identity * coupling
    is_diag = (jnp.arange(NIN) < LB)[None, None, :, None, None]
    return jnp.where(is_diag, symmetric, off_block).astype(jnp.bfloat16)


def draw_bnd_rows(key, part):
    base = jax.random.fold_in(key, 37)
    scores = jax.random.randint(base, (N_SUB, N_ROW, LB), 0, 1 << 20) * LB + jnp.arange(LB, dtype=jnp.int32)
    order = jnp.argsort(scores, axis=-1)
    return order[..., :IFR].astype(jnp.int32)


def draw_if_row(key, part):
    base = jax.random.fold_in(key, 47)
    ladder = jnp.broadcast_to(jnp.arange(LB, dtype=jnp.int32), (N_SUB, N_ROW, NIF))
    return jax.random.permutation(base, ladder, axis=-1, independent=True).astype(jnp.int32)


def draw_if_src(key, part):
    base = jax.random.fold_in(key, 41)
    first_key, second_key = jax.random.split(base)
    quarters = NIF // IFR
    shift_by = jax.random.randint(first_key, (1, N_ROW, quarters, IFR), 1, N_SUB).astype(jnp.int32)
    own_sub = jnp.arange(N_SUB, dtype=jnp.int32)[:, None, None, None]
    target = (own_sub + shift_by) % N_SUB
    ladder = jnp.broadcast_to(jnp.arange(IFR, dtype=jnp.int32), (1, N_ROW, quarters, IFR))
    slot_ids = jax.random.permutation(second_key, ladder, axis=-1, independent=True).astype(jnp.int32)
    return (target * IFR + slot_ids).reshape(N_SUB, N_ROW, NIF).astype(jnp.int32)


def draw_if_val(key, part):
    base = jax.random.fold_in(key, 53)
    first_key, second_key = jax.random.split(base)
    spread = 0.5 / KB
    raw = jax.random.uniform(first_key, (N_SUB, N_ROW, NIF, KB, KB), jnp.float32, -spread, spread)
    coupling = jnp.exp(jax.random.uniform(second_key, (N_SUB, N_ROW, NIF, 1, 1), jnp.float32, math.log(0.75), math.log(2.0)))
    identity = (jnp.arange(KB)[:, None] == jnp.arange(KB)[None, :]).astype(jnp.float32)
    return (raw - identity * coupling).astype(jnp.bfloat16)


def level_of(key, extent, cuts, low, top_value):
    loudness = 1.0
    for position, parts in cuts:
        draws = jax.random.uniform(jax.random.fold_in(jax.random.fold_in(key, 6), position), (parts,), jnp.float32, low / len(cuts), top_value / len(cuts))
        loudness = loudness * jnp.repeat(jnp.exp(draws), extent[position] // parts).reshape((-1,) + (1,) * (len(extent) - 1 - position))
    return loudness


def normal_values(key, shape, scale, most, shards=(), kind=jnp.bfloat16):
    values = jax.random.normal(key, shape, jnp.float32) * scale
    if len(shards) > 0:
        values = level_of(key, shape, shards, -0.22, 0.18) * values
    return jnp.clip(values, min=-most, max=most).astype(kind)


def setup_inputs(seed: int = 0) -> dict:
    key_list = jax.random.split(jax.random.key(seed), 11)
    return {
        "modes": normal_values(key_list[0], (ROWS, NMODE), 1.0, 6.0, ((0, 256),), jnp.float32),
        "search": normal_values(key_list[1], (ROWS, NMODE), 1.0, 6.0, ((0, 256),), jnp.float32),
        "precond": jnp.clip(jnp.exp(math.log(0.25) - 1.609438 * jax.random.uniform(key_list[2], (ROWS,), jnp.float32) ** level_of(key_list[2], (ROWS,), ((0, 256),), -0.2, 0.2)), 0.05, 0.25),
        "in_row": draw_in_row(jax.random.fold_in(key_list[10], 71), 0),
        "in_col": draw_in_col(jax.random.fold_in(key_list[10], 71), 0),
        "in_val": draw_in_val(jax.random.fold_in(key_list[10], 71), 0),
        "bnd_rows": draw_bnd_rows(jax.random.fold_in(key_list[10], 71), 0),
        "if_row": draw_if_row(jax.random.fold_in(key_list[10], 71), 0),
        "if_src": draw_if_src(jax.random.fold_in(key_list[10], 71), 0),
        "if_val": draw_if_val(jax.random.fold_in(key_list[10], 71), 0),
    }


precise_mode = lax.Precision.HIGHEST

def gram_product(left, right):
    return jnp.dot(left.T.astype(jnp.float32), right.astype(jnp.float32), precision=precise_mode, preferred_element_type=jnp.float32)

def full_dot(left, right):
    return jnp.dot(left.astype(jnp.float32), right.astype(jnp.float32), precision=precise_mode, preferred_element_type=jnp.float32)

def chol_solve(matrix, rhs):
    factor = jnp.linalg.cholesky(matrix)
    halfway = lax.linalg.triangular_solve(factor, rhs, left_side=True, lower=True)
    return lax.linalg.triangular_solve(factor, halfway, left_side=True, lower=True, transpose_a=True)

def rescale(factor, moved):
    return lax.linalg.triangular_solve(factor, moved, left_side=False, lower=True, transpose_a=True)

def apply_blocks(vector, in_row, in_col, in_val, bnd_rows, if_row, if_src, if_val):
    width = vector.shape[1]
    pieces = vector.reshape(N_SUB, N_ROW, LB, KB, width)
    row_ids = jnp.arange(N_ROW, dtype=jnp.int32)
    local_ids = jnp.arange(LB, dtype=jnp.int32)

    def subdomain(items):
        group, rows_here, cols_here, vals_here = items
        flat = group.reshape(SUBB, KB, width)
        fetched = flat[cols_here]
        vals_wide = vals_here.astype(jnp.float32)
        forward = jnp.einsum('rkij,rkjw->rkiw', vals_wide, fetched, precision=precise_mode)
        owned = group[row_ids[:, None], rows_here]
        backward = jnp.einsum('rkji,rkjw->rkiw', vals_wide, owned, precision=precise_mode)
        keeper = (cols_here != row_ids[:, None] * LB + rows_here).astype(jnp.float32)
        backward = backward * keeper[:, :, None, None]
        select = (rows_here[:, :, None] == local_ids).astype(jnp.float32)
        result = jnp.einsum('rka,rkiw->raiw', select, forward, precision=precise_mode)
        spread = jax.ops.segment_sum(backward.reshape(N_ROW * NIN, KB, width), cols_here.reshape(-1), num_segments=SUBB)
        return result + spread.reshape(N_ROW, LB, KB, width)
    result = lax.map(subdomain, (pieces, in_row, in_col, in_val))
    sub_ids = jnp.arange(N_SUB, dtype=jnp.int32)[:, None, None]
    row_grid = row_ids[None, :, None]
    boundary = pieces[sub_ids, row_grid, bnd_rows]
    target = (if_src // IFR).astype(jnp.int32)
    slot_ids = (if_src % IFR).astype(jnp.int32)
    remote = boundary[target, row_grid, slot_ids]
    face_wide = if_val.astype(jnp.float32)
    forward = jnp.einsum('srkij,srkjw->srkiw', face_wide, remote, precision=precise_mode)
    owned = pieces[sub_ids, row_grid, if_row]
    backward = jnp.einsum('srkji,srkjw->srkiw', face_wide, owned, precision=precise_mode)
    select = (if_row[..., None] == local_ids).astype(jnp.float32)
    result = result + jnp.einsum('srka,srkiw->sraiw', select, forward, precision=precise_mode)
    destination = ((target * N_ROW + row_grid) * IFR + slot_ids).astype(jnp.int32)
    landed = jax.ops.segment_sum(backward.reshape(-1, KB, width), destination.reshape(-1), num_segments=N_SUB * N_ROW * IFR)
    landed = landed.reshape(N_SUB, N_ROW, IFR, KB, width)
    placed = (bnd_rows[..., None] == local_ids).astype(jnp.float32)
    result = result + jnp.einsum('srqa,srqiw->sraiw', placed, landed, precision=precise_mode)
    return result.reshape(-1, width)

def reference(modes, search, precond, in_row, in_col, in_val, bnd_rows, if_row, if_src, if_val):

    def operator(vector):
        return apply_blocks(vector, in_row, in_col, in_val, bnd_rows, if_row, if_src, if_val)
    nmode = modes.shape[1]
    images = operator(jnp.concatenate([modes, search], 1))
    current, direction = (modes, search)
    image_x, image_p = (images[:, :nmode], images[:, nmode:])
    for sweep in range(ITERS):
        correlation = gram_product(current, current)
        energy = gram_product(current, image_x)
        ritz = chol_solve(correlation, energy)
        residue = image_x - full_dot(current, ritz)
        update = precond[:, None] * residue
        image_w = operator(update)
        basis = jnp.concatenate([update, direction], 1)
        image_b = jnp.concatenate([image_w, image_p], 1)
        coupled = gram_product(basis, image_b)
        driving = gram_product(basis, image_x)
        coeffs = -chol_solve(coupled, driving)
        step_x = full_dot(basis, coeffs)
        step_a = full_dot(image_b, coeffs)
        moved = current + step_x
        moved_image = image_x + step_a
        factor = jnp.linalg.cholesky(gram_product(moved, moved) / ROWS)
        current = rescale(factor, moved)
        image_x = rescale(factor, moved_image)
        direction = rescale(factor, step_x)
        image_p = rescale(factor, step_a)
    return (current, direction)
```

```python
import functools

import jax
import jax.numpy as jnp
from jax import lax
from jax.experimental import pallas as pl
from jax.experimental.pallas import tpu as pltpu
from jax.sharding import PartitionSpec as P

KB = 64
LB = 12
IFR = 3
ITERS = 2
GROUPS = 8
LANES = 128
MESH = pl.DeviceIdType.MESH
F32, BF16 = jnp.float32, jnp.bfloat16
VMEM = pl.BlockSpec(memory_space=pltpu.VMEM)
SMEM = pl.BlockSpec(memory_space=pltpu.SMEM)
ANY = pl.BlockSpec(memory_space=pl.ANY)
LIMIT = 56 * 1024 * 1024


def hdot(a, b):
    return jnp.dot(a, b, precision=lax.Precision.HIGHEST, preferred_element_type=F32)


def swap(v):
    return pltpu.roll(v, LANES // 2, 1)


def is_left(shape):
    return lax.broadcasted_iota(jnp.int32, shape, 1) < LANES // 2


def split3(v):
    hi = v.astype(BF16).astype(F32)
    rest = v - hi
    mid = rest.astype(BF16).astype(F32)
    return hi, mid, (rest - mid).astype(BF16).astype(F32)


def pack(block):
    half = KB // 2
    left = is_left((half, LANES))
    return jnp.where(left, block[:half], swap(block[half:]))


def terms_of(block, width):
    hi, mid, lo = split3(block)
    if width == LANES:
        return jnp.concatenate([hi, mid, lo], 1).astype(BF16)
    left = is_left((KB, LANES))
    return jnp.concatenate(
        [jnp.where(left, hi, swap(mid)), jnp.where(left, lo, 0.0)], 1
    ).astype(BF16)


def sum_terms(total, width):
    if width == LANES:
        return total[:, :LANES] + (total[:, LANES : 2 * LANES] + total[:, 2 * LANES :])
    both = total[:, :LANES] + total[:, LANES:]
    return both + swap(both)


def store_terms(packed, ref, at, width):
    if width == LANES:
        ref[at] = terms_of(packed, width)
        return
    half = KB // 2
    hi, mid, lo = split3(packed)
    left = is_left((half, LANES))
    ref[at, :half, :LANES] = jnp.where(left, hi, swap(mid)).astype(BF16)
    ref[at, :half, LANES:] = jnp.where(left, lo, 0.0).astype(BF16)
    ref[at, half:, :LANES] = jnp.where(left, swap(hi), mid).astype(BF16)
    ref[at, half:, LANES:] = jnp.where(left, swap(lo), 0.0).astype(BF16)


def write_messages(width, basis, out, bnd, face_row, face_src, face_val):
    n_sub = out.shape[0]

    def block_at(row):
        return basis[pl.ds(pl.multiple_of(row * KB, KB), KB), :]

    def sent(block):
        return block if width == LANES else pack(block)

    rows = [sent(block_at(bnd[q])) for q in range(IFR)]

    @pl.loop(0, n_sub)
    def _(t):
        for q in range(IFR):
            out[t, q] = rows[q]
            out[t, IFR + q] = jnp.zeros_like(rows[q])

    @pl.loop(0, LB)
    def _(k):
        terms = terms_of(block_at(face_row[k]), width)
        total = lax.dot_general(
            face_val[k],
            terms,
            (((0,), (0,)), ((), ())),
            preferred_element_type=F32,
        )
        source = face_src[k]
        target, slot = source // IFR, IFR + source % IFR
        out[target, slot] = out[target, slot] + sent(sum_terms(total, width))


def start_kernel(bnd, face_row, face_src, basis, face_val, out):
    write_messages(LANES, basis, out, bnd, face_row, face_src, face_val)


def exchange_kernel(count, ny, nx, n_sub, *refs):
    shards, messages = refs[:count], refs[count]
    groups, received = refs[count + 1 : 2 * count + 1], refs[2 * count + 1]
    local_sem, sub_send, sub_recv, row_send, row_recv = refs[2 * count + 2 :]
    sub, row = lax.axis_index("sub"), lax.axis_index("row")
    y, x = row // nx, row % nx

    def at(dy, dx):
        return ((y + dy + ny) % ny) * nx + (x + dx + nx) % nx

    barrier = pltpu.get_barrier_semaphore()
    for d in range(1, nx):
        pl.semaphore_signal(barrier, inc=1, device_id={"row": at(0, d)}, device_id_type=MESH)
    for d in range(1, ny):
        pl.semaphore_signal(barrier, inc=1, device_id={"row": at(d, 0)}, device_id_type=MESH)
    for d in range(1, n_sub):
        pl.semaphore_signal(barrier, inc=1, device_id={"sub": (sub + d) % n_sub}, device_id_type=MESH)
    pl.semaphore_wait(barrier, nx - 1 + ny - 1 + n_sub - 1)

    own = [pltpu.make_async_copy(shards[i], groups[i].at[row], local_sem.at[i]) for i in range(count)]
    own.append(pltpu.make_async_copy(messages.at[sub], received.at[sub], local_sem.at[count]))

    def hop(i, half, holder, src, to, sem):
        size = shards[i].shape[0] // 2
        return pltpu.make_async_remote_copy(
            src_ref=src,
            dst_ref=groups[i].at[holder, pl.ds(half * size, size)],
            send_sem=row_send.at[i, half, sem],
            recv_sem=row_recv.at[i, half, sem],
            device_id={"row": to},
            device_id_type=MESH,
        )

    def half_of(i, half, holder=None):
        size = shards[i].shape[0] // 2
        part = pl.ds(half * size, size)
        return shards[i].at[part] if holder is None else groups[i].at[holder, part]

    counts = ((nx, ny), (ny, nx))

    def place(half, first, second):
        return at(second, first) if half == 0 else at(first, second)

    sends = []
    for i in range(count):
        for half in range(2):
            n1, n2 = counts[half]
            for first in range(1, n1):
                sends.append(hop(i, half, row, half_of(i, half), place(half, first, 0), first * n2))
                sends[-1].start()
        for half in range(2):
            n1, n2 = counts[half]
            for second in range(1, n2):
                sends.append(hop(i, half, row, half_of(i, half), place(half, 0, second), second))
                sends[-1].start()

    def message(d):
        t = (sub + d) % n_sub
        return pltpu.make_async_remote_copy(
            src_ref=messages.at[t],
            dst_ref=received.at[sub],
            send_sem=sub_send.at[d],
            recv_sem=sub_recv.at[d],
            device_id={"sub": t},
            device_id_type=MESH,
        )

    @pl.loop(1, n_sub)
    def _(d):
        message(d).start()

    for copy in own:
        copy.start()

    def arrived(i, half, holder, sem):
        here = half_of(i, half, holder)
        pltpu.make_async_copy(here, here, row_recv.at[i, half, sem]).wait()

    for i in range(count):
        for first in range(1, max(nx, ny)):
            for half in range(2):
                n1, n2 = counts[half]
                if first >= n1:
                    continue
                holder = place(half, -first, 0)
                arrived(i, half, holder, first * n2)
                for second in range(1, n2):
                    sends.append(
                        hop(i, half, holder, half_of(i, half, holder), place(half, 0, second), first * n2 + second)
                    )
                    sends[-1].start()
    for i in range(count):
        for half in range(2):
            n1, n2 = counts[half]
            for first in range(n1):
                for second in range(1, n2):
                    arrived(i, half, place(half, -first, -second), first * n2 + second)

    @pl.loop(1, n_sub)
    def _(d):
        source = (sub + n_sub - d) % n_sub
        here = received.at[source]
        pltpu.make_async_copy(here, here, sub_recv.at[d]).wait()
        message(d).wait_send()

    for copy in own:
        copy.wait()
    for copy in sends:
        copy.wait_send()


def exchange(collective_id, ny, nx, shards, messages):
    count, n_sub, n_row = len(shards), messages.shape[0], ny * nx
    return pl.pallas_call(
        functools.partial(exchange_kernel, count, ny, nx, n_sub),
        name=f"exchange_{collective_id}",
        out_shape=[jax.ShapeDtypeStruct((n_row, *a.shape), a.dtype) for a in shards]
        + [jax.ShapeDtypeStruct(messages.shape, F32)],
        in_specs=[ANY] * (count + 1),
        out_specs=[ANY] * (count + 1),
        scratch_shapes=[
            pltpu.SemaphoreType.DMA((count + 1,)),
            pltpu.SemaphoreType.DMA((n_sub,)),
            pltpu.SemaphoreType.DMA((n_sub,)),
            pltpu.SemaphoreType.DMA((count, 2, n_row)),
            pltpu.SemaphoreType.DMA((count, 2, n_row)),
        ],
        compiler_params=pltpu.CompilerParams(collective_id=collective_id, has_side_effects=True),
    )(*shards, messages)


def sum_kernel(n_sub, n_row, parts, out, by_row, by_sub, own_sem, send, recv):
    sub, row = lax.axis_index("sub"), lax.axis_index("row")
    barrier = pltpu.get_barrier_semaphore()

    @pl.loop(1, n_row)
    def _(d):
        pl.semaphore_signal(barrier, inc=1, device_id={"row": (row + d) % n_row}, device_id_type=MESH)

    @pl.loop(1, n_sub)
    def _(d):
        pl.semaphore_signal(barrier, inc=1, device_id={"sub": (sub + d) % n_sub}, device_id_type=MESH)

    pl.semaphore_wait(barrier, n_row - 1 + n_sub - 1)

    def phase(index, axis, mine, n, source, target):
        def to(d):
            t = (mine + d) % n
            return pltpu.make_async_remote_copy(
                src_ref=source(t),
                dst_ref=target(mine),
                send_sem=send.at[index, d],
                recv_sem=recv.at[index, d],
                device_id={axis: t},
                device_id_type=MESH,
            )

        own = pltpu.make_async_copy(source(mine), target(mine), own_sem.at[index])

        @pl.loop(1, n)
        def _(d):
            to(d).start()

        own.start()

        @pl.loop(1, n)
        def _(d):
            here = target((mine + n - d) % n)
            pltpu.make_async_copy(here, here, recv.at[index, d]).wait()
            to(d).wait_send()

        own.wait()

    def summed(buffer, n):
        total = buffer[0]
        for t in range(1, n):
            total = total + buffer[t]
        return total

    phase(0, "row", row, n_row, lambda t: parts.at[t], lambda t: by_row.at[t])
    by_row[n_row] = summed(by_row, n_row)
    phase(1, "sub", sub, n_sub, lambda t: by_row.at[n_row], lambda t: by_sub.at[t])
    by_sub[n_sub] = summed(by_sub, n_sub)
    phase(2, "row", row, n_row, lambda t: by_sub.at[n_sub], lambda t: out.at[t])


def sum_all(collective_id, n_sub, n_row, part):
    rows = part.shape[0] // n_row
    most = max(n_sub, n_row)
    shape = (n_row, rows, LANES)
    total = pl.pallas_call(
        functools.partial(sum_kernel, n_sub, n_row),
        name=f"sum_{collective_id}",
        out_shape=jax.ShapeDtypeStruct(shape, F32),
        in_specs=[VMEM],
        out_specs=VMEM,
        scratch_shapes=[
            pltpu.VMEM((n_row + 1, rows, LANES), F32),
            pltpu.VMEM((n_sub + 1, rows, LANES), F32),
            pltpu.SemaphoreType.DMA((3,)),
            pltpu.SemaphoreType.DMA((3, most)),
            pltpu.SemaphoreType.DMA((3, most)),
        ],
        compiler_params=pltpu.CompilerParams(collective_id=collective_id, has_side_effects=True),
    )(part.reshape(shape))
    return total.reshape(part.shape)


def build_kernel(own_at, back_at, face_at, own_val, all_val, face_val, rows_ref):
    half = KB // 2
    left = is_left((half, LANES))

    def pair(one, two):
        top = jnp.where(left, one, swap(two))
        low = jnp.where(left, swap(one), two)
        return jnp.concatenate([top, low], 0)

    def put(a, slot, value):
        rows_ref[a, :, slot * LANES : (slot + 1) * LANES] = value.astype(BF16)

    @pl.loop(0, LB)
    def _(a):
        for g in range(0, GROUPS, 2):
            one, two = (own_val[own_at[a * GROUPS + g + i]].astype(F32) for i in range(2))
            put(a, g // 2, pair(one, two))
        back = [all_val[back_at[a * (GROUPS - 1) + g]].astype(F32) for g in range(GROUPS - 1)]
        turned = jnp.concatenate([pair(back[0], back[2]), pair(back[1], back[3])], 0).T
        put(a, 4, turned[:KB])
        put(a, 5, turned[KB:])
        turned = jnp.concatenate([pair(back[4], back[6]), pair(back[5], back[5])], 0).T
        put(a, 6, turned[:KB])
        face = face_val[face_at[a]].astype(F32)
        put(a, 7, jnp.where(is_left((KB, LANES)), turned[KB:], jnp.concatenate([face, face], 1)))


def apply_operator(width, col_at, bnd, rows_ref, group, received, terms, put_row):
    n_group, n_sub = group.shape[0], received.shape[0]

    @pl.loop(0, n_group)
    def _(j):
        store_terms(group[j], terms, j, width)

    @pl.loop(0, n_sub)
    def _(t):
        for q in range(IFR):
            store_terms(received[t, q], terms, n_group + t * IFR + q, width)

    step = 4
    slots = 2 * GROUPS

    @pl.loop(0, LB)
    def _(a):
        total = None
        for c in range(slots // step):
            stack = jnp.concatenate([terms[col_at[a * slots + c * step + i]] for i in range(step)], 0)
            part = jnp.dot(
                rows_ref[a, :, c * step * KB : (c + 1) * step * KB], stack, preferred_element_type=F32
            )
            total = part if total is None else total + part
        put_row(a, sum_terms(total, width))


def landed_block(width, received, q):
    n_sub = received.shape[0]
    total = received[0, IFR + q]
    for t in range(1, n_sub):
        total = total + received[t, IFR + q]
    if width == LANES:
        return total
    left = is_left(total.shape)
    other = swap(total)
    return jnp.concatenate([jnp.where(left, total, other), jnp.where(left, other, total)], 0)


def first_apply_kernel(col_at, bnd, rows_ref, group, received, basis, image, gram, terms):
    def put_row(a, block):
        image[pl.ds(pl.multiple_of(a * KB, KB), KB), :] = block

    apply_operator(LANES, col_at, bnd, rows_ref, group, received, terms, put_row)
    for q in range(IFR):
        at = pl.ds(pl.multiple_of(bnd[q] * KB, KB), KB)
        image[at, :] = image[at, :] + landed_block(LANES, received, q)
    both = basis[...]
    left = is_left(both.shape)
    gram[...] = hdot(both.T, jnp.where(left, both, swap(image[...])))


def apply_kernel(col_at, bnd, rows_ref, group, received, current, image_x, basis, image_b, gram, terms):
    left_block = is_left((KB, LANES))

    def put_row(a, block):
        at = pl.ds(pl.multiple_of(a * KB, KB), KB)
        image_b[at, :] = jnp.where(left_block, block, image_x[at, :])

    apply_operator(KB, col_at, bnd, rows_ref, group, received, terms, put_row)
    for q in range(IFR):
        at = pl.ds(pl.multiple_of(bnd[q] * KB, KB), KB)
        block = landed_block(KB, received, q)
        image_b[at, :] = image_b[at, :] + jnp.where(left_block, block, 0.0)
    y = basis[...]
    turned = y.T
    left = is_left(y.shape)
    gram[0:LANES] = hdot(turned, image_b[...])
    gram[LANES : 2 * LANES] = hdot(turned, jnp.where(left, image_x[...], swap(current[...])))
    gram[2 * LANES :] = hdot(turned, y)


def eliminate(work, n, full):
    shape = (n, LANES)
    lane = lax.broadcasted_iota(jnp.int32, shape, 1)
    line = lax.broadcasted_iota(jnp.int32, (n, 1), 0)
    lane1 = lax.broadcasted_iota(jnp.int32, (1, LANES), 1)

    def step(j, pivots):
        row = work[pl.ds(j, 1), :]
        pivot = jnp.sum(jnp.where(lane1 == j, row[:, :LANES], 0.0), axis=1, keepdims=True)
        whole = work[...]
        column = jnp.sum(jnp.where(lane == j, whole[:, :LANES], 0.0), axis=1, keepdims=True)
        scaled = row * (1.0 / pivot)
        if full:
            work[...] = jnp.where(line == j, scaled, whole - column * scaled)
        else:
            work[...] = whole - jnp.where(line > j, column, 0.0) * scaled
        return jnp.where(line == j, pivot, pivots)

    return lax.fori_loop(0, n, step, jnp.zeros((n, 1), F32))


def rest_of(shape):
    return is_left(shape)


def padded(top):
    return jnp.concatenate([top, jnp.zeros_like(top)], 0)


def identity_right():
    line = lax.broadcasted_iota(jnp.int32, (KB, LANES), 0)
    lane = lax.broadcasted_iota(jnp.int32, (KB, LANES), 1)
    return (lane == line + KB).astype(F32)


def identity_left():
    line = lax.broadcasted_iota(jnp.int32, (KB, LANES), 0)
    lane = lax.broadcasted_iota(jnp.int32, (KB, LANES), 1)
    return (lane == line).astype(F32)


CHUNK = 256


def chunks(body):
    @pl.loop(0, LB * KB // CHUNK)
    def _(c):
        body(pl.ds(pl.multiple_of(c * CHUNK, CHUNK), CHUNK))


def new_basis(ritz, precond, current, image_x, basis, update, at):
    here = current[at, :]
    left = is_left(here.shape)
    residue = jnp.where(left, image_x[at, :], 0.0) - hdot(here, ritz)
    fresh = precond[at, :] * residue
    update[at, :] = fresh
    basis[at, :] = jnp.where(left, fresh, here)


def send_basis(update, packed, messages, bnd, face_row, face_src, face_val):
    @pl.loop(0, LB)
    def _(a):
        packed[a] = pack(update[pl.ds(pl.multiple_of(a * KB, KB), KB), :])

    write_messages(KB, update, messages, bnd, face_row, face_src, face_val)


def first_ritz_kernel(
    bnd, face_row, face_src, gram, face_val, precond, current, image_x, basis, packed, messages, update, work
):
    work[...] = gram[:KB]
    eliminate(work, KB, True)
    left = is_left((KB, LANES))
    ritz = padded(jnp.where(left, swap(work[...]), 0.0))
    chunks(lambda at: new_basis(ritz, precond, current, image_x, basis, update, at))
    send_basis(update, packed, messages, bnd, face_row, face_src, face_val)


def combine(total_rows, gram, metric, wide, narrow):
    wide[:, :LANES] = gram[0:LANES]
    right = gram[LANES : 2 * LANES]
    wide[:, LANES:] = right
    eliminate(wide, LANES, True)
    left_all = is_left((LANES, LANES))
    left = is_left((KB, LANES))
    z = jnp.where(left_all, -wide[:, LANES:], 0.0)
    cross = hdot(right.T, z)
    against = jnp.where(left_all, swap(right), 0.0) + hdot(gram[2 * LANES :], z)
    square = hdot(z.T, against)[:KB]
    lengths = jnp.where(left, metric[...], 0.0) + cross[KB:] + square
    narrow[...] = lengths * (1.0 / total_rows) + identity_right()
    pivots = eliminate(narrow, KB, False)
    root = 1.0 / jnp.sqrt(pivots)
    inverse = padded(jnp.where(left, swap(narrow[...]), 0.0) * root)
    turned = inverse.T
    half = hdot(z, turned)
    energy = jnp.where(left, swap(metric[...]), 0.0) + cross[:KB]
    energy = hdot(hdot(inverse, padded(energy)), turned)
    return turned, jnp.where(left_all, half, swap(half)), energy


def step_kernel(
    total_rows,
    bnd,
    face_row,
    face_src,
    gram,
    metric,
    face_val,
    precond,
    current,
    image_x,
    basis,
    image_b,
    next_metric,
    next_current,
    next_image,
    next_basis,
    packed,
    messages,
    update,
    wide,
    narrow,
):
    turned, moves, energy = combine(total_rows, gram, metric, wide, narrow)
    next_metric[...] = identity_left() * total_rows + swap(energy[:KB])
    ritz = energy * (1.0 / total_rows)

    def body(at):
        next_current[at, :] = hdot(current[at, :], turned) + hdot(basis[at, :], moves)
        next_image[at, :] = hdot(image_x[at, :], turned) + hdot(image_b[at, :], moves)
        new_basis(ritz, precond, next_current, next_image, next_basis, update, at)

    chunks(body)
    send_basis(update, packed, messages, bnd, face_row, face_src, face_val)


def last_kernel(total_rows, gram, metric, current, basis, modes, search, wide, narrow):
    turned, moves, _ = combine(total_rows, gram, metric, wide, narrow)

    def body(at):
        both = hdot(current[at, :], turned) + hdot(basis[at, :], moves)
        modes[at, :] = both[:, :KB]
        search[at, :] = swap(both)[:, :KB]

    chunks(body)


def plain(kernel, name, specs, outs, scratch, *args):
    return pl.pallas_call(
        kernel,
        name=name,
        out_shape=outs,
        in_specs=specs,
        out_specs=[VMEM] * len(outs),
        scratch_shapes=scratch,
        compiler_params=pltpu.CompilerParams(vmem_limit_bytes=LIMIT),
    )(*args)


def shape(*dims):
    return jax.ShapeDtypeStruct(dims, F32)


def tables(n_row, in_row, in_col, if_row, if_src):
    row = lax.axis_index("row")
    everyone = lax.all_gather(jnp.stack([in_row, in_col]), "row")
    own_ids = jnp.arange(LB, dtype=jnp.int32)
    k_ids = jnp.arange(GROUPS * LB, dtype=jnp.int32).reshape(GROUPS, LB)
    hit = in_row.reshape(GROUPS, LB)[None] == own_ids[:, None, None]
    own_at = jnp.sum(jnp.where(hit, k_ids[None], 0), 2)
    own_col = jnp.sum(jnp.where(hit, in_col.reshape(GROUPS, LB)[None], 0), 2)
    rows_all = everyone[:, 0, LB:].reshape(n_row, GROUPS - 1, LB)
    cols_all = everyone[:, 1, LB:].reshape(n_row, GROUPS - 1, LB)
    r_ids = jnp.arange(n_row, dtype=jnp.int32)[:, None, None]
    back_hit = cols_all[None] == (row * LB + own_ids)[:, None, None, None]
    back_k = r_ids * ((GROUPS - 1) * LB) + (k_ids[1:] - LB)[None]
    back_at = jnp.sum(jnp.where(back_hit, back_k[None], 0), (1, 3))
    back_col = jnp.sum(jnp.where(back_hit, (r_ids * LB + rows_all)[None], 0), (1, 3))
    face_hit = if_row[None] == own_ids[:, None]
    face_at = jnp.sum(jnp.where(face_hit, own_ids[None], 0), 1)
    face_col = n_row * LB + jnp.sum(jnp.where(face_hit, if_src[None], 0), 1)
    col_at = jnp.concatenate([own_col, back_col, face_col[:, None]], 1)
    return own_at.reshape(-1), back_at.reshape(-1), face_at, col_at.reshape(-1)


def local(grid, modes, search, precond, in_row, in_col, in_val, bnd_rows, if_row, if_src, if_val):
    n_sub, ny, nx = grid
    n_row = ny * nx
    rows_here = LB * KB
    total_rows = float(rows_here * n_sub * n_row)
    bnd, face_row, face_src, face_val = bnd_rows[0, 0], if_row[0, 0], if_src[0, 0], if_val[0, 0]
    own_at, back_at, face_at, col_at = tables(n_row, in_row[0, 0], in_col[0, 0], face_row, face_src)
    vals = in_val[0, 0]
    half = KB // 2
    own_val = jnp.concatenate([vals[:, :half], vals[:, half:]], 2)
    weights = jnp.broadcast_to(precond[:, None], (rows_here, LANES))
    current = jnp.concatenate([modes, search], 1)

    (messages,) = plain(
        start_kernel,
        "start",
        [SMEM] * 3 + [VMEM] * 2,
        [shape(n_sub, 2 * IFR, KB, LANES)],
        [],
        bnd,
        face_row,
        face_src,
        current,
        face_val,
    )
    group, all_val, received = exchange(
        0, ny, nx, [current, own_val[LB:].reshape(-1, LANES)], messages
    )
    block_rows = pl.pallas_call(
        build_kernel,
        name="build",
        out_shape=jax.ShapeDtypeStruct((LB, KB, 2 * GROUPS * KB), BF16),
        in_specs=[SMEM] * 3 + [VMEM] * 3,
        out_specs=VMEM,
        compiler_params=pltpu.CompilerParams(vmem_limit_bytes=LIMIT),
    )(own_at, back_at, face_at, own_val, all_val.reshape(-1, half, LANES), face_val)
    blocks_all = n_row * LB + n_sub * IFR
    image_x, gram = plain(
        first_apply_kernel,
        "first_apply",
        [SMEM] * 2 + [VMEM] * 4,
        [shape(rows_here, LANES), shape(LANES, LANES)],
        [pltpu.VMEM((blocks_all, KB, 3 * LANES), BF16)],
        col_at,
        bnd,
        block_rows,
        group.reshape(-1, KB, LANES),
        received,
        current,
    )
    metric = sum_all(1, n_sub, n_row, gram)
    sent = [shape(rows_here, LANES), shape(LB, half, LANES), shape(n_sub, 2 * IFR, half, LANES)]
    basis, packed, messages = plain(
        first_ritz_kernel,
        "first_ritz",
        [SMEM] * 3 + [VMEM] * 5,
        sent,
        [pltpu.VMEM((rows_here, LANES), F32), pltpu.VMEM((KB, LANES), F32)],
        bnd,
        face_row,
        face_src,
        metric,
        face_val,
        weights,
        current,
        image_x,
    )
    metric = metric[:KB]
    for sweep in range(ITERS):
        group, received = exchange(2 + 2 * sweep, ny, nx, [packed.reshape(-1, LANES)], messages)
        image_b, gram = plain(
            apply_kernel,
            "apply",
            [SMEM] * 2 + [VMEM] * 6,
            [shape(rows_here, LANES), shape(3 * LANES, LANES)],
            [pltpu.VMEM((blocks_all, KB, 2 * LANES), BF16)],
            col_at,
            bnd,
            block_rows,
            group.reshape(-1, half, LANES),
            received,
            current,
            image_x,
            basis,
        )
        gram = sum_all(3 + 2 * sweep, n_sub, n_row, gram)
        solver = [pltpu.VMEM((LANES, 2 * LANES), F32), pltpu.VMEM((KB, LANES), F32)]
        if sweep < ITERS - 1:
            metric, current, image_x, basis, packed, messages = plain(
                functools.partial(step_kernel, total_rows),
                "step",
                [SMEM] * 3 + [VMEM] * 8,
                [shape(KB, LANES), shape(rows_here, LANES), shape(rows_here, LANES), *sent],
                [pltpu.VMEM((rows_here, LANES), F32), *solver],
                bnd,
                face_row,
                face_src,
                gram,
                metric,
                face_val,
                weights,
                current,
                image_x,
                basis,
                image_b,
            )
    return plain(
        functools.partial(last_kernel, total_rows),
        "last",
        [VMEM] * 4,
        [shape(rows_here, KB), shape(rows_here, KB)],
        solver,
        gram,
        metric,
        current,
        basis,
    )


def solution(mesh):
    n_sub, n_row = mesh.shape["sub"], mesh.shape["row"]
    ny = 4 if n_row == 16 else 2
    return jax.shard_map(
        functools.partial(local, (n_sub, ny, n_row // ny)),
        mesh=mesh,
        in_specs=(
            P(("sub", "row"), None),
            P(("sub", "row"), None),
            P(("sub", "row")),
            P("sub", "row", None),
            P("sub", "row", None),
            P("sub", "row", None, None, None),
            P("sub", "row", None),
            P("sub", "row", None),
            P("sub", "row", None),
            P("sub", "row", None, None, None),
        ),
        out_specs=(P(("sub", "row"), None), P(("sub", "row"), None)),
        check_vma=False,
    )
```

```python
import functools

import jax
import jax.numpy as jnp
from jax import lax
from jax.experimental import pallas as pl
from jax.experimental.pallas import tpu as pltpu
from jax.sharding import PartitionSpec as P

KB = 64
LB = 12
IFR = 3
ITERS = 2
GROUPS = 8
HALF = KB // 2
SLOTS = 2 * GROUPS
LANES = 128
MESH = pl.DeviceIdType.MESH
F32, BF16 = jnp.float32, jnp.bfloat16
VMEM = pl.BlockSpec(memory_space=pltpu.VMEM)
SMEM = pl.BlockSpec(memory_space=pltpu.SMEM)
ANY = pl.BlockSpec(memory_space=pl.ANY)
LIMIT = 40 * 1024 * 1024
EARLY = 4 * LB


def hdot(a, b):
    return jnp.dot(a, b, precision=lax.Precision.HIGHEST, preferred_element_type=F32)


def swap(v):
    return pltpu.roll(v, LANES // 2, 1)


def is_left(shape):
    return lax.broadcasted_iota(jnp.int32, shape, 1) < LANES // 2


def pack(block):
    left = is_left((HALF, LANES))
    return jnp.where(left, block[:HALF], swap(block[HALF:]))


def two_terms(v):
    hi = v.astype(BF16)
    return hi, (v - hi.astype(F32)).astype(BF16)


def write_messages(many, shard, bnd_out, parts, bnd, face_row, face_src, face_val):
    for q in range(IFR):
        bnd_out[q] = shard[bnd[0, 0, q]]
    parts[...] = jnp.zeros_like(parts)
    left = is_left((HALF, LANES))
    products = []
    for k in range(LB):
        block = shard[face_row[0, 0, k]]
        face = face_val[0, 0, k]
        terms = []
        for v in range(many):
            terms.extend(two_terms(block[v * HALF : (v + 1) * HALF]))
        terms = jnp.concatenate(terms, 1)
        one, two = (
            lax.dot_general(half, terms, (((0,), (0,)), ((), ())), preferred_element_type=F32)
            for half in (face[:HALF], face[HALF:])
        )
        sums = []
        for v in range(many):
            at = 2 * v * LANES
            first = one[:, at : at + LANES] + one[:, at + LANES : at + 2 * LANES]
            second = two[:, at : at + LANES] + two[:, at + LANES : at + 2 * LANES]
            sums.append(
                jnp.where(left, first[:HALF] + swap(second[:HALF]), swap(first[HALF:]) + second[HALF:])
            )
        products.append(jnp.concatenate(sums, 0) if many > 1 else sums[0])
    for k in range(LB):
        source = face_src[0, 0, k]
        target, slot = source // IFR, source % IFR
        core, z = target % 2, target // 2
        parts[core, z, slot] = parts[core, z, slot] + products[k]


def start_kernel(bnd, face_row, face_src, modes, search, precond, face_val, current, shard, bnd_out, parts, weights):
    current[...] = jnp.concatenate([modes[...], search[...]], 0).T
    for a in range(LB):
        block = current[a * KB : (a + 1) * KB]
        shard[a, :HALF] = pack(block)
        shard[a, HALF:] = pack(swap(block))
    for c in range(LB * KB // LANES):
        weights[c * LANES : (c + 1) * LANES] = jnp.broadcast_to(precond[c : c + 1], (LANES, LANES)).T
    write_messages(2, shard, bnd_out, parts, bnd, face_row, face_src, face_val)


def exchange_kernel(count, rings, ny, nx, n_sub, *refs):
    arrays = count + 2 * rings
    shards, bnd, parts = refs[:arrays], refs[arrays], refs[arrays + 1]
    groups, bnd_all, landed = refs[arrays + 2 : 2 * arrays + 2], refs[2 * arrays + 2], refs[2 * arrays + 3]
    theirs, ours, sub_send, sub_recv, row_send, row_recv, ring_send, ring_recv = refs[2 * arrays + 4 :]
    sub, row = lax.axis_index("sub"), lax.axis_index("row")
    y, x = row // nx, row % nx
    nz = n_sub // 2
    z, core = sub // 2, sub % 2
    sibling = z * 2 + 1 - core

    def at(dy, dx):
        return ((y + dy + ny) % ny) * nx + (x + dx + nx) % nx

    def along(d):
        return ((z + d + nz) % nz) * 2 + core

    barrier = pltpu.get_barrier_semaphore()
    for d in range(1, nx):
        pl.semaphore_signal(barrier, inc=1, device_id={"row": at(0, d)}, device_id_type=MESH)
    for d in range(1, ny):
        pl.semaphore_signal(barrier, inc=1, device_id={"row": at(d, 0)}, device_id_type=MESH)
    for d in range(1, nz):
        pl.semaphore_signal(barrier, inc=1, device_id={"sub": along(d)}, device_id_type=MESH)
    pl.semaphore_signal(barrier, inc=1, device_id={"sub": sibling}, device_id_type=MESH)
    pl.semaphore_wait(barrier, nx - 1 + ny - 1 + nz)

    def to_sub(src, dst, kind, d, target):
        return pltpu.make_async_remote_copy(
            src_ref=src,
            dst_ref=dst,
            send_sem=sub_send.at[kind, d],
            recv_sem=sub_recv.at[kind, d],
            device_id={"sub": target},
            device_id_type=MESH,
        )

    def landed_at(ref, sem):
        pltpu.make_async_copy(ref, ref, sem).wait()

    def hop(i, half, holder, src, to, sem):
        size = shards[i].shape[0] // 2
        return pltpu.make_async_remote_copy(
            src_ref=src,
            dst_ref=groups[i].at[holder, pl.ds(half * size, size)],
            send_sem=row_send.at[i, half, sem],
            recv_sem=row_recv.at[i, half, sem],
            device_id={"row": to},
            device_id_type=MESH,
        )

    def half_of(i, half, holder=None):
        size = shards[i].shape[0] // 2
        part = pl.ds(half * size, size)
        return shards[i].at[part] if holder is None else groups[i].at[holder, part]

    counts = ((nx, ny), (ny, nx))

    def place(half, first, second):
        return at(second, first) if half == 0 else at(first, second)

    sends = []

    def send(copy):
        copy.start()
        sends.append(copy)

    send(to_sub(parts.at[1 - core], theirs, 3, 0, sibling))
    for i in range(count):
        for half in range(2):
            n1, n2 = counts[half]
            for first in range(1, n1):
                send(hop(i, half, row, half_of(i, half), place(half, first, 0), first * n2))
        if i == 0:
            for d in range(1, nz):
                send(to_sub(bnd, bnd_all.at[sub], 0, d, along(d)))
            send(to_sub(bnd, bnd_all.at[sub], 1, 0, sibling))
        for half in range(2):
            n1, n2 = counts[half]
            for second in range(1, n2):
                send(hop(i, half, row, half_of(i, half), place(half, 0, second), second))

    for axis in range(2 * rings):
        mine = (x, y)[axis]
        for d in range(1, counts[axis][0]):
            send(
                pltpu.make_async_remote_copy(
                    src_ref=shards[count + axis],
                    dst_ref=groups[count + axis].at[mine],
                    send_sem=ring_send.at[axis, d],
                    recv_sem=ring_recv.at[axis, d],
                    device_id={"row": place(axis, d, 0)},
                    device_id_type=MESH,
                )
            )

    landed_at(theirs, sub_recv.at[3, 0])
    ours[...] = theirs[...] + parts[core]
    for d in range(1, nz):
        send(to_sub(ours.at[(z + d) % nz], landed.at[z], 2, d, along(d)))
    landed[z] = ours[z]

    for i in range(count):
        for first in range(1, max(nx, ny)):
            for half in range(2):
                n1, n2 = counts[half]
                if first >= n1:
                    continue
                holder = place(half, -first, 0)
                landed_at(half_of(i, half, holder), row_recv.at[i, half, first * n2])
                for second in range(1, n2):
                    send(hop(i, half, holder, half_of(i, half, holder), place(half, 0, second), first * n2 + second))
        if i == 0:
            for d in range(1, nz):
                here = bnd_all.at[along(-d)]
                landed_at(here, sub_recv.at[0, d])
                send(to_sub(here, here, 1, d, sibling))
    for d in range(1, nz):
        landed_at(landed.at[(z + nz - d) % nz], sub_recv.at[2, d])
    for d in range(nz):
        landed_at(bnd_all.at[((z + nz - d) % nz) * 2 + 1 - core], sub_recv.at[1, d])
    for i in range(count):
        for half in range(2):
            n1, n2 = counts[half]
            for first in range(n1):
                for second in range(1, n2):
                    landed_at(half_of(i, half, place(half, -first, -second)), row_recv.at[i, half, first * n2 + second])
    for axis in range(2 * rings):
        mine, n = (x, y)[axis], counts[axis][0]
        for d in range(1, n):
            landed_at(groups[count + axis].at[(mine + n - d) % n], ring_recv.at[axis, d])
    for copy in sends:
        copy.wait_send()


def exchange(collective_id, ny, nx, shards, rings, bnd, parts):
    count, n_row = len(shards), ny * nx
    nz = parts.shape[1]
    n_sub = 2 * nz
    most = max(nz, 2)
    gathered = [jax.ShapeDtypeStruct((n_row, *a.shape), a.dtype) for a in shards]
    gathered += [jax.ShapeDtypeStruct((n, *a.shape), a.dtype) for n, a in zip((nx, ny), rings)]
    return pl.pallas_call(
        functools.partial(exchange_kernel, count, bool(rings), ny, nx, n_sub),
        name=f"exchange_{collective_id}",
        out_shape=gathered
        + [jax.ShapeDtypeStruct((n_sub, *bnd.shape), F32), jax.ShapeDtypeStruct(parts.shape[1:], F32)],
        in_specs=[VMEM] * (len(gathered) + 2),
        out_specs=[VMEM] * (len(gathered) + 2),
        scratch_shapes=[
            pltpu.VMEM(parts.shape[1:], F32),
            pltpu.VMEM(parts.shape[1:], F32),
            pltpu.SemaphoreType.DMA((4, most)),
            pltpu.SemaphoreType.DMA((4, most)),
            pltpu.SemaphoreType.DMA((count, 2, n_row)),
            pltpu.SemaphoreType.DMA((count, 2, n_row)),
            pltpu.SemaphoreType.DMA((2, max(nx, ny))),
            pltpu.SemaphoreType.DMA((2, max(nx, ny))),
        ],
        compiler_params=pltpu.CompilerParams(
            collective_id=collective_id, has_side_effects=True, vmem_limit_bytes=LIMIT
        ),
    )(*shards, *rings, bnd, parts)


def hand_on_kernel(ny, nx, to_y, to_x, from_y, from_x, send, recv):
    row = lax.axis_index("row")
    y, x = row // nx, row % nx
    axes = ((ny, y, lambda t: t * nx + x, to_y, from_y), (nx, x, lambda t: y * nx + t, to_x, from_x))
    barrier = pltpu.get_barrier_semaphore()
    for n, mine, name, _, _ in axes:
        for d in range(1, n):
            pl.semaphore_signal(barrier, inc=1, device_id={"row": name((mine + d) % n)}, device_id_type=MESH)
    pl.semaphore_wait(barrier, ny - 1 + nx - 1)
    sends = []
    for i, (n, mine, name, src, dst) in enumerate(axes):
        for d in range(1, n):
            t = (mine + d) % n
            copy = pltpu.make_async_remote_copy(
                src_ref=src.at[t],
                dst_ref=dst.at[mine],
                send_sem=send.at[i, d],
                recv_sem=recv.at[i, d],
                device_id={"row": name(t)},
                device_id_type=MESH,
            )
            copy.start()
            sends.append(copy)
    for i, (n, mine, _, _, dst) in enumerate(axes):
        for d in range(1, n):
            here = dst.at[(mine + n - d) % n]
            pltpu.make_async_copy(here, here, recv.at[i, d]).wait()
    for copy in sends:
        copy.wait_send()


def hand_on(collective_id, ny, nx, to_y, to_x):
    return pl.pallas_call(
        functools.partial(hand_on_kernel, ny, nx),
        name=f"hand_on_{collective_id}",
        out_shape=[
            jax.ShapeDtypeStruct((ny, *to_y.shape[1:]), BF16),
            jax.ShapeDtypeStruct((nx, *to_x.shape[1:]), BF16),
        ],
        in_specs=[VMEM] * 2,
        out_specs=[VMEM] * 2,
        scratch_shapes=[pltpu.SemaphoreType.DMA((2, max(nx, ny)))] * 2,
        compiler_params=pltpu.CompilerParams(
            collective_id=collective_id, has_side_effects=True, vmem_limit_bytes=LIMIT
        ),
    )(to_y, to_x)


def sum_kernel(n_sub, n_row, parts, out, by_row, by_sub, own_sem, send, recv):
    sub, row = lax.axis_index("sub"), lax.axis_index("row")
    barrier = pltpu.get_barrier_semaphore()

    @pl.loop(1, n_row)
    def _(d):
        pl.semaphore_signal(barrier, inc=1, device_id={"row": (row + d) % n_row}, device_id_type=MESH)

    @pl.loop(1, n_sub)
    def _(d):
        pl.semaphore_signal(barrier, inc=1, device_id={"sub": (sub + d) % n_sub}, device_id_type=MESH)

    pl.semaphore_wait(barrier, n_row - 1 + n_sub - 1)

    def phase(index, axis, mine, n, source, target):
        def to(d):
            t = (mine + d) % n
            return pltpu.make_async_remote_copy(
                src_ref=source(t),
                dst_ref=target(mine),
                send_sem=send.at[index, d],
                recv_sem=recv.at[index, d],
                device_id={axis: t},
                device_id_type=MESH,
            )

        own = pltpu.make_async_copy(source(mine), target(mine), own_sem.at[index])

        @pl.loop(1, n)
        def _(d):
            to(d).start()

        own.start()

        @pl.loop(1, n)
        def _(d):
            here = target((mine + n - d) % n)
            pltpu.make_async_copy(here, here, recv.at[index, d]).wait()
            to(d).wait_send()

        own.wait()

    def summed(buffer, n):
        total = buffer[0]
        for t in range(1, n):
            total = total + buffer[t]
        return total

    phase(0, "row", row, n_row, lambda t: parts.at[t], lambda t: by_row.at[t])
    by_row[n_row] = summed(by_row, n_row)
    phase(1, "sub", sub, n_sub, lambda t: by_row.at[n_row], lambda t: by_sub.at[t])
    by_sub[n_sub] = summed(by_sub, n_sub)
    phase(2, "row", row, n_row, lambda t: by_sub.at[n_sub], lambda t: out.at[t])


def sum_all(collective_id, n_sub, n_row, part):
    rows = part.shape[0] // n_row
    most = max(n_sub, n_row)
    shape = (n_row, rows, LANES)
    total = pl.pallas_call(
        functools.partial(sum_kernel, n_sub, n_row),
        name=f"sum_{collective_id}",
        out_shape=jax.ShapeDtypeStruct(shape, F32),
        in_specs=[VMEM],
        out_specs=VMEM,
        scratch_shapes=[
            pltpu.VMEM((n_row + 1, rows, LANES), F32),
            pltpu.VMEM((n_sub + 1, rows, LANES), F32),
            pltpu.SemaphoreType.DMA((3,)),
            pltpu.SemaphoreType.DMA((3, most)),
            pltpu.SemaphoreType.DMA((3, most)),
        ],
        compiler_params=pltpu.CompilerParams(collective_id=collective_id, has_side_effects=True),
    )(part.reshape(shape))
    return total.reshape(part.shape)


def select_kernel(ny, nx, code_at, codes, own_val, ring_x, ring_y, to_y, to_x, back_at):
    row = lax.axis_index("row")
    y, x = row // nx, row % nx

    def scatter(device, source, start, size, out, n, mine_of, place_of, mine):
        @pl.loop(0, size // LB)
        def _(g):
            for b in range(LB):
                k = g * LB + b
                code = code_at[device, start + k]
                owner = code // 256
                slot = g * LB + code // 16 % 16
                out[jnp.where(mine_of(owner) == mine, place_of(owner), n), slot] = source(k)

    late = LB * GROUPS - LB - EARLY

    def by_x(device, source):
        scatter(device, source, LB, EARLY, to_y, ny, lambda o: o % nx, lambda o: o // nx, x)

    def by_y(device, source):
        scatter(device, source, LB + EARLY, late, to_x, nx, lambda o: o // nx, lambda o: o % nx, y)

    by_x(row, lambda k: own_val[LB + k])
    by_y(row, lambda k: own_val[LB + EARLY + k])

    @pl.loop(1, nx)
    def _(d):
        t = (x + d) % nx
        by_x(y * nx + t, lambda k: ring_x[t, k])

    @pl.loop(1, ny)
    def _(d):
        t = (y + d) % ny
        by_y(t * nx + x, lambda k: ring_y[t, k])

    code = codes[...]
    lane = lax.broadcasted_iota(jnp.int32, code.shape, 1)
    device = lax.broadcasted_iota(jnp.int32, code.shape, 0)
    ours = (code // 256 == row) & (lane >= LB) & (lane < GROUPS * LB)
    value = device * 16 + code % 16
    place = code // 16 % 16
    lines = [jnp.sum(jnp.where(ours & (place == a), value, 0), axis=0, keepdims=True) for a in range(LB)]
    lines += [jnp.zeros_like(lines[0])] * (16 - LB)
    k = lax.broadcasted_iota(jnp.int32, (LANES, LANES), 0)
    g = lax.broadcasted_iota(jnp.int32, (LANES, LANES), 1)
    member = ((k >= g * LB) & (k < g * LB + LB)).astype(F32)
    back_at[...] = hdot(jnp.concatenate(lines, 0).astype(F32), member).astype(jnp.int32)


def build_kernel(
    ny, nx, in_row, in_col, back_at, face_row, face_src, own_val, to_y, to_x, from_y, from_x, face_val, rows_ref, col_at,
    own_at, face_at
):
    n_row = ny * nx
    row = lax.axis_index("row")
    y, x = row // nx, row % nx

    @pl.loop(0, GROUPS)
    def _(g):
        for b in range(LB):
            k = g * LB + b
            own_at[g * LB + in_row[0, 0, k]] = k

    for k in range(LB):
        face_at[face_row[0, 0, k]] = k

    quarter = lax.broadcasted_iota(jnp.int32, (KB, LANES), 1) % KB < HALF
    left = is_left((HALF, LANES))

    def pair(one, two):
        top = jnp.where(left, one, swap(two))
        low = jnp.where(left, swap(one), two)
        return jnp.concatenate([top, low], 0)

    @pl.loop(0, LB)
    def _(a):
        def put(slot, ij, kl):
            lanes = slice(slot * LANES, (slot + 1) * LANES)
            rows_ref[a, :KB, lanes] = jnp.where(quarter, ij, pltpu.roll(kl, HALF, 1)).astype(BF16)
            rows_ref[a, KB:, lanes] = jnp.where(quarter, pltpu.roll(ij, LANES - HALF, 1), kl).astype(BF16)

        own = []
        for g in range(GROUPS):
            k = own_at[g * LB + a]
            col_at[a * SLOTS + g] = in_col[0, 0, k]
            own.append(own_val[k].astype(F32))
        put(0, pair(own[0], own[2]), pair(own[1], own[3]))
        put(1, pair(own[4], own[6]), pair(own[5], own[7]))
        back = []
        for g in range(GROUPS - 1):
            code = back_at[a, g + 1]
            device = code // 16
            col_at[a * SLOTS + GROUPS + g] = device * LB + code % 16
            if (g + 1) * LB <= EARLY:
                slot, t, mine, kept, got = g * LB + a, device // nx, y, to_y, from_y
            else:
                slot, t, mine, kept, got = g * LB - EARLY + a, device % nx, x, to_x, from_x
            back.append(jnp.where(t == mine, kept[mine, slot].astype(F32), got[t, slot].astype(F32)))
        turned = jnp.concatenate([pair(back[0], back[1]), pair(back[2], back[3])], 0).T
        put(2, turned[:KB], turned[KB:])
        turned = jnp.concatenate([pair(back[4], back[5]), pair(back[6], back[6])], 0).T
        k = face_at[a]
        col_at[a * SLOTS + SLOTS - 1] = n_row * LB + face_src[0, 0, k]
        face = face_val[0, 0, k].astype(F32)
        put(3, turned[:KB], jnp.where(is_left((KB, LANES)), turned[KB:], jnp.concatenate([face, face], 1)))


def apply_operator(many, col_at, rows_ref, own, group, bnd_all, terms, put_row):
    n_row, n_sub = group.shape[0], bnd_all.shape[0]

    def split(values, at, size):
        for v in range(many):
            hi, mid = two_terms(values[:, v * HALF : (v + 1) * HALF])
            lane = 2 * v * LANES
            terms[pl.ds(at, size), :, lane : lane + LANES] = hi
            terms[pl.ds(at, size), :, lane + LANES : lane + 2 * LANES] = mid

    @pl.loop(0, n_row)
    def _(r):
        split(group[r], r * LB, LB)

    split(own[...], lax.axis_index("row") * LB, LB)

    @pl.loop(0, n_sub)
    def _(t):
        split(bnd_all[t], n_row * LB + t * IFR, IFR)

    together = 3

    @pl.loop(0, LB // together)
    def _(c):
        for i in range(together):
            a = c * together + i
            total = None
            for part in range(2):
                here = range(part * GROUPS, (part + 1) * GROUPS)
                stack = jnp.concatenate([terms[col_at[a * SLOTS + t]] for t in here], 0)
                lhs = rows_ref[a, :, part * GROUPS * HALF : (part + 1) * GROUPS * HALF]
                product = jnp.dot(lhs, stack, preferred_element_type=F32)
                total = product if total is None else total + product
            blocks = []
            for v in range(many):
                lane = 2 * v * LANES
                both = total[:, lane : lane + LANES] + total[:, lane + LANES : lane + 2 * LANES]
                blocks.append(both[:KB] + swap(both[KB:]))
            put_row(a, blocks)


def landed_blocks(many, landed, q):
    total = landed[0, q]
    for t in range(1, landed.shape[0]):
        total = total + landed[t, q]
    parts = [total[v * HALF : (v + 1) * HALF] for v in range(many)]
    return [jnp.concatenate([part, swap(part)], 0) for part in parts]


def block_at(a):
    return pl.ds(pl.multiple_of(a * KB, KB), KB)


def first_apply_kernel(col_at, bnd, rows_ref, own, group, bnd_all, landed, basis, image, gram, terms):
    left_block = is_left((KB, LANES))

    def put_row(a, blocks):
        image[block_at(a), :] = jnp.where(left_block, blocks[0], swap(blocks[1]))

    apply_operator(2, col_at, rows_ref, own, group, bnd_all, terms, put_row)
    for q in range(IFR):
        one, two = landed_blocks(2, landed, q)
        at = block_at(bnd[0, 0, q])
        image[at, :] = image[at, :] + jnp.where(left_block, one, swap(two))
    both = basis[...]
    left = is_left(both.shape)
    gram[...] = hdot(both.T, jnp.where(left, both, swap(image[...])))


def apply_kernel(col_at, bnd, rows_ref, own, group, bnd_all, landed, current, image_x, basis, image_b, gram, terms):
    left_block = is_left((KB, LANES))

    def put_row(a, blocks):
        at = block_at(a)
        image_b[at, :] = jnp.where(left_block, blocks[0], image_x[at, :])

    apply_operator(1, col_at, rows_ref, own, group, bnd_all, terms, put_row)
    for q in range(IFR):
        at = block_at(bnd[0, 0, q])
        image_b[at, :] = image_b[at, :] + jnp.where(left_block, landed_blocks(1, landed, q)[0], 0.0)
    y = basis[...]
    turned = y.T
    left = is_left(y.shape)
    gram[0:LANES] = hdot(turned, image_b[...])
    gram[LANES : 2 * LANES] = hdot(turned, jnp.where(left, image_x[...], swap(current[...])))
    gram[2 * LANES :] = hdot(turned, y)


def eliminate(work, n, full):
    lane = lax.broadcasted_iota(jnp.int32, (n, LANES), 1)
    line = lax.broadcasted_iota(jnp.int32, (n, 1), 0)
    lane1 = lax.broadcasted_iota(jnp.int32, (1, LANES), 1)

    def step(t, pivots):
        j = 2 * t
        k = j + 1
        row0, row1 = work[pl.ds(j, 1), :], work[pl.ds(k, 1), :]
        whole = work[...]

        def entry(row, at):
            return jnp.sum(jnp.where(lane1 == at, row[:, :LANES], 0.0), axis=1, keepdims=True)

        def column(at):
            return jnp.sum(jnp.where(lane == at, whole[:, :LANES], 0.0), axis=1, keepdims=True)

        a, b, c, d = entry(row0, j), entry(row0, k), entry(row1, j), entry(row1, k)
        col0, col1 = column(j), column(k)
        inverse = 1.0 / a
        ratio = b * inverse
        below = row1 - (c * inverse) * row0
        second = d - c * ratio
        unit1 = below * (1.0 / second)
        unit0 = row0 * inverse - ratio * unit1
        moved = whole - (col0 * unit0 + col1 * unit1)
        if full:
            work[...] = jnp.where(line == j, unit0, jnp.where(line == k, unit1, moved))
        else:
            work[...] = jnp.where(line > k, moved, jnp.where(line == k, below, whole))
        return jnp.where(line == j, a, jnp.where(line == k, second, pivots))

    return lax.fori_loop(0, n // 2, step, jnp.zeros((n, 1), F32))


def padded(top):
    return jnp.concatenate([top, jnp.zeros_like(top)], 0)


def identity_right():
    line = lax.broadcasted_iota(jnp.int32, (KB, LANES), 0)
    lane = lax.broadcasted_iota(jnp.int32, (KB, LANES), 1)
    return (lane == line + KB).astype(F32)


def identity_left():
    line = lax.broadcasted_iota(jnp.int32, (KB, LANES), 0)
    lane = lax.broadcasted_iota(jnp.int32, (KB, LANES), 1)
    return (lane == line).astype(F32)


CHUNK = 256


def chunks(body):
    @pl.loop(0, LB * KB // CHUNK)
    def _(c):
        body(pl.ds(pl.multiple_of(c * CHUNK, CHUNK), CHUNK))


def new_basis(ritz, precond, current, image_x, basis, update, at):
    here = current[at, :]
    left = is_left(here.shape)
    residue = jnp.where(left, image_x[at, :], 0.0) - hdot(here, ritz)
    fresh = precond[at, :] * residue
    update[at, :] = fresh
    basis[at, :] = jnp.where(left, fresh, here)


def send_basis(update, packed, bnd_out, parts, bnd, face_row, face_src, face_val):
    for a in range(LB):
        packed[a] = pack(update[a * KB : (a + 1) * KB, :])
    write_messages(1, packed, bnd_out, parts, bnd, face_row, face_src, face_val)


def first_ritz_kernel(
    bnd, face_row, face_src, gram, face_val, precond, current, image_x, basis, packed, bnd_out, parts, update, work
):
    work[...] = gram[:KB]
    eliminate(work, KB, True)
    left = is_left((KB, LANES))
    ritz = padded(jnp.where(left, swap(work[...]), 0.0))
    chunks(lambda at: new_basis(ritz, precond, current, image_x, basis, update, at))
    send_basis(update, packed, bnd_out, parts, bnd, face_row, face_src, face_val)


def combine(total_rows, gram, metric, wide, narrow):
    wide[:, :LANES] = gram[0:LANES]
    right = gram[LANES : 2 * LANES]
    wide[:, LANES:] = right
    eliminate(wide, LANES, True)
    left_all = is_left((LANES, LANES))
    left = is_left((KB, LANES))
    z = jnp.where(left_all, -wide[:, LANES:], 0.0)
    cross = hdot(right.T, z)
    against = jnp.where(left_all, swap(right), 0.0) + hdot(gram[2 * LANES :], z)
    square = hdot(z.T, against)[:KB]
    lengths = jnp.where(left, metric[...], 0.0) + cross[KB:] + square
    narrow[...] = lengths * (1.0 / total_rows) + identity_right()
    pivots = eliminate(narrow, KB, False)
    root = 1.0 / jnp.sqrt(pivots)
    inverse = padded(jnp.where(left, swap(narrow[...]), 0.0) * root)
    turned = inverse.T
    half = hdot(z, turned)
    energy = jnp.where(left, swap(metric[...]), 0.0) + cross[:KB]
    energy = hdot(hdot(inverse, padded(energy)), turned)
    return turned, jnp.where(left_all, half, swap(half)), energy


def step_kernel(
    total_rows,
    bnd,
    face_row,
    face_src,
    gram,
    metric,
    face_val,
    precond,
    current,
    image_x,
    basis,
    image_b,
    next_metric,
    next_current,
    next_image,
    next_basis,
    packed,
    bnd_out,
    parts,
    update,
    wide,
    narrow,
):
    turned, moves, energy = combine(total_rows, gram, metric, wide, narrow)
    next_metric[...] = identity_left() * total_rows + swap(energy[:KB])
    ritz = energy * (1.0 / total_rows)

    def body(at):
        next_current[at, :] = hdot(current[at, :], turned) + hdot(basis[at, :], moves)
        next_image[at, :] = hdot(image_x[at, :], turned) + hdot(image_b[at, :], moves)
        new_basis(ritz, precond, next_current, next_image, next_basis, update, at)

    chunks(body)
    send_basis(update, packed, bnd_out, parts, bnd, face_row, face_src, face_val)


def last_kernel(total_rows, gram, metric, current, basis, modes, search, both, wide, narrow):
    turned, moves, _ = combine(total_rows, gram, metric, wide, narrow)

    def body(at):
        both[at, :] = hdot(current[at, :], turned) + hdot(basis[at, :], moves)

    chunks(body)
    whole = both[...].T
    modes[...] = whole[:KB]
    search[...] = whole[KB:]


def plain(kernel, name, specs, outs, scratch, *args):
    return pl.pallas_call(
        kernel,
        name=name,
        out_shape=outs,
        in_specs=specs,
        out_specs=[VMEM] * len(outs),
        scratch_shapes=scratch,
        compiler_params=pltpu.CompilerParams(vmem_limit_bytes=LIMIT),
    )(*args)


def shape(*dims):
    return jax.ShapeDtypeStruct(dims, F32)


def local(grid, modes, search, precond, in_row, in_col, in_val, bnd_rows, if_row, if_src, if_val):
    n_sub, ny, nx = grid
    n_row = ny * nx
    rows_here = LB * KB
    total_rows = float(rows_here * n_sub * n_row)
    vals = in_val[0, 0]
    own_val = jnp.concatenate([vals[:, :HALF], vals[:, HALF:]], 2)
    faces = (bnd_rows, if_row, if_src)

    def sent(many):
        return [
            shape(LB, many * HALF, LANES),
            shape(IFR, many * HALF, LANES),
            shape(2, n_sub // 2, IFR, many * HALF, LANES),
        ]

    current, shard, bnd, parts, weights = plain(
        start_kernel,
        "start",
        [SMEM] * 3 + [VMEM] * 4,
        [shape(rows_here, LANES), *sent(2), shape(rows_here, LANES)],
        [],
        *faces,
        modes.T,
        search.T,
        precond.reshape(-1, LANES),
        if_val,
    )
    cols = in_col[0]
    codes = cols // LB * 256 + cols % LB * 16 + in_row[0]
    codes = jnp.pad(codes, ((0, 15), (0, LANES - GROUPS * LB)))
    early = own_val[LB : LB + EARLY].reshape(-1, LANES)
    late = own_val[LB + EARLY :].reshape(-1, LANES)
    group, codes_all, ring_x, ring_y, bnd_all, landed = exchange(
        0, ny, nx, [shard.reshape(-1, LANES), codes], [early, late], bnd, parts
    )
    codes_all = lax.dynamic_update_slice(codes_all[:, 0], codes[:1], (lax.axis_index("row"), 0))
    in_early, in_late = EARLY, GROUPS * LB - LB - EARLY

    def blocks(n, count):
        return jax.ShapeDtypeStruct((n, count, HALF, LANES), BF16)

    to_y, to_x, back_at = plain(
        functools.partial(select_kernel, ny, nx),
        "select",
        [SMEM] + [VMEM] * 4,
        [blocks(ny + 1, in_early), blocks(nx + 1, in_late), jax.ShapeDtypeStruct((16, LANES), jnp.int32)],
        [],
        codes_all,
        codes_all,
        own_val,
        ring_x.reshape(nx, in_early, HALF, LANES),
        ring_y.reshape(ny, in_late, HALF, LANES),
    )
    from_y, from_x = hand_on(6, ny, nx, to_y, to_x)
    block_rows, col_at = pl.pallas_call(
        functools.partial(build_kernel, ny, nx),
        name="build",
        out_shape=[
            jax.ShapeDtypeStruct((LB, 2 * KB, SLOTS * HALF), BF16),
            jax.ShapeDtypeStruct((LB * SLOTS,), jnp.int32),
        ],
        in_specs=[SMEM] * 5 + [VMEM] * 6,
        out_specs=[VMEM, SMEM],
        scratch_shapes=[pltpu.SMEM((GROUPS * LB,), jnp.int32), pltpu.SMEM((LB,), jnp.int32)],
        compiler_params=pltpu.CompilerParams(vmem_limit_bytes=LIMIT),
    )(in_row, in_col, back_at, if_row, if_src, own_val, to_y, to_x, from_y, from_x, if_val)
    blocks_all = n_row * LB + n_sub * IFR
    image_x, gram = plain(
        first_apply_kernel,
        "first_apply",
        [SMEM] * 2 + [VMEM] * 6,
        [shape(rows_here, LANES), shape(LANES, LANES)],
        [pltpu.VMEM((blocks_all, HALF, 4 * LANES), BF16)],
        col_at,
        bnd_rows,
        block_rows,
        shard,
        group.reshape(n_row, LB, 2 * HALF, LANES),
        bnd_all,
        landed,
        current,
    )
    metric = sum_all(1, n_sub, n_row, gram)
    basis, packed, bnd, parts = plain(
        first_ritz_kernel,
        "first_ritz",
        [SMEM] * 3 + [VMEM] * 5,
        [shape(rows_here, LANES), *sent(1)],
        [pltpu.VMEM((rows_here, LANES), F32), pltpu.VMEM((KB, LANES), F32)],
        *faces,
        metric,
        if_val,
        weights,
        current,
        image_x,
    )
    metric = metric[:KB]
    solver = [pltpu.VMEM((rows_here, LANES), F32), pltpu.VMEM((LANES, 2 * LANES), F32), pltpu.VMEM((KB, LANES), F32)]
    for sweep in range(ITERS):
        group, bnd_all, landed = exchange(2 + 2 * sweep, ny, nx, [packed.reshape(-1, LANES)], [], bnd, parts)
        image_b, gram = plain(
            apply_kernel,
            "apply",
            [SMEM] * 2 + [VMEM] * 8,
            [shape(rows_here, LANES), shape(3 * LANES, LANES)],
            [pltpu.VMEM((blocks_all, HALF, 2 * LANES), BF16)],
            col_at,
            bnd_rows,
            block_rows,
            packed,
            group.reshape(n_row, LB, HALF, LANES),
            bnd_all,
            landed,
            current,
            image_x,
            basis,
        )
        gram = sum_all(3 + 2 * sweep, n_sub, n_row, gram)
        if sweep < ITERS - 1:
            metric, current, image_x, basis, packed, bnd, parts = plain(
                functools.partial(step_kernel, total_rows),
                "step",
                [SMEM] * 3 + [VMEM] * 8,
                [shape(KB, LANES), shape(rows_here, LANES), shape(rows_here, LANES), shape(rows_here, LANES), *sent(1)],
                solver,
                *faces,
                gram,
                metric,
                if_val,
                weights,
                current,
                image_x,
                basis,
                image_b,
            )
    modes, search = plain(
        functools.partial(last_kernel, total_rows),
        "last",
        [VMEM] * 4,
        [shape(KB, rows_here), shape(KB, rows_here)],
        solver,
        gram,
        metric,
        current,
        basis,
    )
    return modes.T, search.T


def solution(mesh):
    n_sub, n_row = mesh.shape["sub"], mesh.shape["row"]
    ny = 4 if n_row == 16 else 2
    return jax.shard_map(
        functools.partial(local, (n_sub, ny, n_row // ny)),
        mesh=mesh,
        in_specs=(
            P(("sub", "row"), None),
            P(("sub", "row"), None),
            P(("sub", "row")),
            P("sub", "row", None),
            P("sub", "row", None),
            P("sub", "row", None, None, None),
            P("sub", "row", None),
            P("sub", "row", None),
            P("sub", "row", None),
            P("sub", "row", None, None, None),
        ),
        out_specs=(P(("sub", "row"), None), P(("sub", "row"), None)),
        check_vma=False,
    )
```

```python
import functools

import jax
import jax.numpy as jnp
from jax import lax
from jax.experimental import pallas as pl
from jax.experimental.pallas import tpu as pltpu
from jax.sharding import PartitionSpec as P

KB = 64
LB = 12
IFR = 3
ITERS = 2
GROUPS = 8
HALF = KB // 2
SLOTS = 2 * GROUPS
LANES = 128
MESH = pl.DeviceIdType.MESH
F32, BF16 = jnp.float32, jnp.bfloat16
VMEM = pl.BlockSpec(memory_space=pltpu.VMEM)
SMEM = pl.BlockSpec(memory_space=pltpu.SMEM)
ANY = pl.BlockSpec(memory_space=pl.ANY)
LIMIT = 12 * 1024 * 1024
SMALL = 4 * 1024 * 1024
EARLY = 4 * LB


def hdot(a, b):
    return jnp.dot(a, b, precision=lax.Precision.HIGHEST, preferred_element_type=F32)


def swap(v):
    return pltpu.roll(v, LANES // 2, 1)


def is_left(shape):
    return lax.broadcasted_iota(jnp.int32, shape, 1) < LANES // 2


def pack(block):
    left = is_left((HALF, LANES))
    return jnp.where(left, block[:HALF], swap(block[HALF:]))


def two_terms(v):
    hi = v.astype(BF16)
    return hi, (v - hi.astype(F32)).astype(BF16)


def add_terms(coarse, product, v):
    if coarse:
        return product
    at = 2 * v * LANES
    return product[:, at : at + LANES] + product[:, at + LANES : at + 2 * LANES]


def write_messages(many, coarse, shard, bnd_out, parts, bnd, face_row, face_src, face_val):
    for q in range(IFR):
        bnd_out[q] = shard[bnd[0, 0, q]]
    parts[...] = jnp.zeros_like(parts)
    left = is_left((HALF, LANES))
    products = []
    for k in range(LB):
        block = shard[face_row[0, 0, k]]
        face = face_val[0, 0, k]
        if coarse:
            terms = block
        else:
            terms = jnp.concatenate([t for v in range(many) for t in two_terms(block[v * HALF : (v + 1) * HALF])], 1)
        one, two = (
            lax.dot_general(half, terms, (((0,), (0,)), ((), ())), preferred_element_type=F32)
            for half in (face[:HALF], face[HALF:])
        )
        sums = []
        for v in range(many):
            first, second = add_terms(coarse, one, v), add_terms(coarse, two, v)
            sums.append(
                jnp.where(left, first[:HALF] + swap(second[:HALF]), swap(first[HALF:]) + second[HALF:])
            )
        products.append(jnp.concatenate(sums, 0) if many > 1 else sums[0])
    for k in range(LB):
        source = face_src[0, 0, k]
        target, slot = source // IFR, source % IFR
        core, z = target % 2, target // 2
        parts[core, z, slot] = parts[core, z, slot] + products[k]


def start_kernel(bnd, face_row, face_src, modes, search, precond, face_val, current, shard, bnd_out, parts, weights):
    current[...] = jnp.concatenate([modes[...], search[...]], 0).T
    for a in range(LB):
        block = current[a * KB : (a + 1) * KB]
        shard[a, :HALF] = pack(block)
        shard[a, HALF:] = pack(swap(block))
    for c in range(LB * KB // LANES):
        weights[c * LANES : (c + 1) * LANES] = jnp.broadcast_to(precond[c : c + 1], (LANES, LANES)).T
    write_messages(2, False, shard, bnd_out, parts, bnd, face_row, face_src, face_val)


def exchange_kernel(count, handing, ny, nx, n_sub, *refs):
    arrays = count + 2 * handing
    shards, bnd, parts = refs[:arrays], refs[arrays], refs[arrays + 1]
    groups, bnd_all, landed = refs[arrays + 2 : 2 * arrays + 2], refs[2 * arrays + 2], refs[2 * arrays + 3]
    theirs, ours, sub_send, sub_recv, row_send, row_recv, ring_send, ring_recv = refs[2 * arrays + 4 :]
    sub, row = lax.axis_index("sub"), lax.axis_index("row")
    y, x = row // nx, row % nx
    nz = n_sub // 2
    z, core = sub // 2, sub % 2
    sibling = z * 2 + 1 - core

    def at(dy, dx):
        return ((y + dy + ny) % ny) * nx + (x + dx + nx) % nx

    def along(d):
        return ((z + d + nz) % nz) * 2 + core

    barrier = pltpu.get_barrier_semaphore()
    for d in range(1, nx):
        pl.semaphore_signal(barrier, inc=1, device_id={"row": at(0, d)}, device_id_type=MESH)
    for d in range(1, ny):
        pl.semaphore_signal(barrier, inc=1, device_id={"row": at(d, 0)}, device_id_type=MESH)
    for d in range(1, nz):
        pl.semaphore_signal(barrier, inc=1, device_id={"sub": along(d)}, device_id_type=MESH)
    pl.semaphore_signal(barrier, inc=1, device_id={"sub": sibling}, device_id_type=MESH)
    pl.semaphore_wait(barrier, nx - 1 + ny - 1 + nz)

    def to_sub(src, dst, kind, d, target):
        return pltpu.make_async_remote_copy(
            src_ref=src,
            dst_ref=dst,
            send_sem=sub_send.at[kind, d],
            recv_sem=sub_recv.at[kind, d],
            device_id={"sub": target},
            device_id_type=MESH,
        )

    def landed_at(ref, sem):
        pltpu.make_async_copy(ref, ref, sem).wait()

    def hop(i, half, holder, src, to, sem):
        size = shards[i].shape[0] // 2
        return pltpu.make_async_remote_copy(
            src_ref=src,
            dst_ref=groups[i].at[holder, pl.ds(half * size, size)],
            send_sem=row_send.at[i, half, sem],
            recv_sem=row_recv.at[i, half, sem],
            device_id={"row": to},
            device_id_type=MESH,
        )

    def half_of(i, half, holder=None):
        size = shards[i].shape[0] // 2
        part = pl.ds(half * size, size)
        return shards[i].at[part] if holder is None else groups[i].at[holder, part]

    counts = ((nx, ny), (ny, nx))

    def place(half, first, second):
        return at(second, first) if half == 0 else at(first, second)

    sends = []

    def send(copy):
        copy.start()
        sends.append(copy)

    send(to_sub(parts.at[1 - core], theirs, 3, 0, sibling))
    for i in range(count):
        for half in range(2):
            n1, n2 = counts[half]
            for first in range(1, n1):
                send(hop(i, half, row, half_of(i, half), place(half, first, 0), first * n2))
        if i == 0:
            for d in range(1, nz):
                send(to_sub(bnd, bnd_all.at[sub], 0, d, along(d)))
            send(to_sub(bnd, bnd_all.at[sub], 1, 0, sibling))
        for half in range(2):
            n1, n2 = counts[half]
            for second in range(1, n2):
                send(hop(i, half, row, half_of(i, half), place(half, 0, second), second))

    for axis in range(2 * handing):
        mine, n = (y, x)[axis], (ny, nx)[axis]
        for d in range(1, n):
            t = (mine + d) % n
            send(
                pltpu.make_async_remote_copy(
                    src_ref=shards[count + axis].at[t],
                    dst_ref=groups[count + axis].at[mine],
                    send_sem=ring_send.at[axis, d],
                    recv_sem=ring_recv.at[axis, d],
                    device_id={"row": (t * nx + x, y * nx + t)[axis]},
                    device_id_type=MESH,
                )
            )

    landed_at(theirs, sub_recv.at[3, 0])
    ours[...] = theirs[...] + parts[core]
    for d in range(1, nz):
        send(to_sub(ours.at[(z + d) % nz], landed.at[z], 2, d, along(d)))
    landed[z] = ours[z]

    for i in range(count):
        for first in range(1, max(nx, ny)):
            for half in range(2):
                n1, n2 = counts[half]
                if first >= n1:
                    continue
                holder = place(half, -first, 0)
                landed_at(half_of(i, half, holder), row_recv.at[i, half, first * n2])
                for second in range(1, n2):
                    send(hop(i, half, holder, half_of(i, half, holder), place(half, 0, second), first * n2 + second))
        if i == 0:
            for d in range(1, nz):
                here = bnd_all.at[along(-d)]
                landed_at(here, sub_recv.at[0, d])
                send(to_sub(here, here, 1, d, sibling))
    for d in range(1, nz):
        landed_at(landed.at[(z + nz - d) % nz], sub_recv.at[2, d])
    for d in range(nz):
        landed_at(bnd_all.at[((z + nz - d) % nz) * 2 + 1 - core], sub_recv.at[1, d])
    for i in range(count):
        for half in range(2):
            n1, n2 = counts[half]
            for first in range(n1):
                for second in range(1, n2):
                    landed_at(half_of(i, half, place(half, -first, -second)), row_recv.at[i, half, first * n2 + second])
    for axis in range(2 * handing):
        mine, n = (y, x)[axis], (ny, nx)[axis]
        for d in range(1, n):
            landed_at(groups[count + axis].at[(mine + n - d) % n], ring_recv.at[axis, d])
    for copy in sends:
        copy.wait_send()


def exchange(collective_id, ny, nx, shards, handed, bnd, parts):
    count, n_row = len(shards), ny * nx
    nz = parts.shape[1]
    n_sub = 2 * nz
    most = max(nz, 2)
    gathered = [jax.ShapeDtypeStruct((n_row, *a.shape), a.dtype) for a in shards]
    gathered += [jax.ShapeDtypeStruct((n, *a.shape[1:]), a.dtype) for n, a in zip((ny, nx), handed)]
    return pl.pallas_call(
        functools.partial(exchange_kernel, count, bool(handed), ny, nx, n_sub),
        name=f"exchange_{collective_id}",
        out_shape=gathered
        + [jax.ShapeDtypeStruct((n_sub, *bnd.shape), bnd.dtype), jax.ShapeDtypeStruct(parts.shape[1:], F32)],
        in_specs=[VMEM] * (len(gathered) + 2),
        out_specs=[VMEM] * (len(gathered) + 2),
        scratch_shapes=[
            pltpu.VMEM(parts.shape[1:], F32),
            pltpu.VMEM(parts.shape[1:], F32),
            pltpu.SemaphoreType.DMA((4, most)),
            pltpu.SemaphoreType.DMA((4, most)),
            pltpu.SemaphoreType.DMA((count, 2, n_row)),
            pltpu.SemaphoreType.DMA((count, 2, n_row)),
            pltpu.SemaphoreType.DMA((2, max(nx, ny))),
            pltpu.SemaphoreType.DMA((2, max(nx, ny))),
        ],
        compiler_params=pltpu.CompilerParams(
            collective_id=collective_id, has_side_effects=True, vmem_limit_bytes=SMALL
        ),
    )(*shards, *handed, bnd, parts)


def rings_kernel(ny, nx, codes, early, late, codes_all, ring_x, ring_y, send, recv):
    row = lax.axis_index("row")
    y, x = row // nx, row % nx
    n_row = ny * nx
    barrier = pltpu.get_barrier_semaphore()
    for d in range(1, n_row):
        pl.semaphore_signal(barrier, inc=1, device_id={"row": (row + d) % n_row}, device_id_type=MESH)
    pl.semaphore_wait(barrier, n_row - 1)
    rings = (
        (nx, x, lambda t: y * nx + t, early, ring_x),
        (ny, y, lambda t: t * nx + x, late, ring_y),
        (n_row, row, lambda t: t, codes, codes_all),
    )
    sends = []
    for i, (n, mine, name, src, dst) in enumerate(rings):
        for d in range(1, n):
            copy = pltpu.make_async_remote_copy(
                src_ref=src,
                dst_ref=dst.at[mine],
                send_sem=send.at[i, d],
                recv_sem=recv.at[i, d],
                device_id={"row": name((mine + d) % n)},
                device_id_type=MESH,
            )
            copy.start()
            sends.append(copy)
    codes_all[row] = codes[...]
    for i, (n, mine, _, _, dst) in enumerate(rings):
        for d in range(1, n):
            here = dst.at[(mine + n - d) % n]
            pltpu.make_async_copy(here, here, recv.at[i, d]).wait()
    for copy in sends:
        copy.wait_send()


def ring_gather(collective_id, ny, nx, codes, early, late):
    return pl.pallas_call(
        functools.partial(rings_kernel, ny, nx),
        name=f"rings_{collective_id}",
        out_shape=[
            jax.ShapeDtypeStruct((n, *a.shape), a.dtype) for n, a in ((ny * nx, codes), (nx, early), (ny, late))
        ],
        in_specs=[VMEM] * 3,
        out_specs=[VMEM] * 3,
        scratch_shapes=[pltpu.SemaphoreType.DMA((3, ny * nx))] * 2,
        compiler_params=pltpu.CompilerParams(
            collective_id=collective_id, has_side_effects=True, vmem_limit_bytes=SMALL
        ),
    )(codes, early, late)


def sum_kernel(n_sub, n_row, parts, out, by_row, by_sub, own_sem, send, recv):
    sub, row = lax.axis_index("sub"), lax.axis_index("row")
    barrier = pltpu.get_barrier_semaphore()

    @pl.loop(1, n_row)
    def _(d):
        pl.semaphore_signal(barrier, inc=1, device_id={"row": (row + d) % n_row}, device_id_type=MESH)

    @pl.loop(1, n_sub)
    def _(d):
        pl.semaphore_signal(barrier, inc=1, device_id={"sub": (sub + d) % n_sub}, device_id_type=MESH)

    pl.semaphore_wait(barrier, n_row - 1 + n_sub - 1)

    def phase(index, axis, mine, n, source, target):
        def to(d):
            t = (mine + d) % n
            return pltpu.make_async_remote_copy(
                src_ref=source(t),
                dst_ref=target(mine),
                send_sem=send.at[index, d],
                recv_sem=recv.at[index, d],
                device_id={axis: t},
                device_id_type=MESH,
            )

        own = pltpu.make_async_copy(source(mine), target(mine), own_sem.at[index])

        @pl.loop(1, n)
        def _(d):
            to(d).start()

        own.start()

        @pl.loop(1, n)
        def _(d):
            here = target((mine + n - d) % n)
            pltpu.make_async_copy(here, here, recv.at[index, d]).wait()
            to(d).wait_send()

        own.wait()

    def summed(buffer, n):
        total = buffer[0]
        for t in range(1, n):
            total = total + buffer[t]
        return total

    phase(0, "row", row, n_row, lambda t: parts.at[t], lambda t: by_row.at[t])
    by_row[n_row] = summed(by_row, n_row)
    phase(1, "sub", sub, n_sub, lambda t: by_row.at[n_row], lambda t: by_sub.at[t])
    by_sub[n_sub] = summed(by_sub, n_sub)
    phase(2, "row", row, n_row, lambda t: by_sub.at[n_sub], lambda t: out.at[t])


def sum_all(collective_id, n_sub, n_row, part):
    rows = part.shape[0] // n_row
    most = max(n_sub, n_row)
    shape = (n_row, rows, LANES)
    total = pl.pallas_call(
        functools.partial(sum_kernel, n_sub, n_row),
        name=f"sum_{collective_id}",
        out_shape=jax.ShapeDtypeStruct(shape, F32),
        in_specs=[VMEM],
        out_specs=VMEM,
        scratch_shapes=[
            pltpu.VMEM((n_row + 1, rows, LANES), F32),
            pltpu.VMEM((n_sub + 1, rows, LANES), F32),
            pltpu.SemaphoreType.DMA((3,)),
            pltpu.SemaphoreType.DMA((3, most)),
            pltpu.SemaphoreType.DMA((3, most)),
        ],
        compiler_params=pltpu.CompilerParams(
            collective_id=collective_id, has_side_effects=True, vmem_limit_bytes=SMALL
        ),
    )(part.reshape(shape))
    return total.reshape(part.shape)


def select_kernel(ny, nx, codes, own_val, ring_x, ring_y, to_y, to_x, back_at, flat, goes, goes_at, sem):
    row = lax.axis_index("row")
    y, x = row // nx, row % nx
    late = LB * GROUPS - LB - EARLY
    flat[...] = codes[:, 0, :]
    value = flat[...]
    owner, within = value // 256, value // 16 % 16
    at = lax.broadcasted_iota(jnp.int32, value.shape, 1)
    member = jnp.zeros_like(at)
    for g in range(1, GROUPS):
        member = member + jnp.where(at >= g * LB, LB, 0)
    by_x = jnp.where(owner % nx == x, owner // nx, ny) * EARLY + member - LB + within
    by_y = jnp.where(owner // nx == y, owner % nx, nx) * late + member - LB - EARLY + within
    goes[...] = jnp.where(at < LB + EARLY, by_x, by_y)
    copy = pltpu.make_async_copy(goes, goes_at, sem)
    copy.start()
    copy.wait()

    def scatter(device, source, start, size, out):
        @pl.loop(0, size // LB)
        def _(g):
            for b in range(LB):
                k = g * LB + b
                out[goes_at[device, start + k]] = source(k)

    scatter(row, lambda k: own_val[LB + k], LB, EARLY, to_y)
    scatter(row, lambda k: own_val[LB + EARLY + k], LB + EARLY, late, to_x)

    @pl.loop(1, nx)
    def _(d):
        t = (x + d) % nx
        scatter(y * nx + t, lambda k: ring_x[t, k], LB, EARLY, to_y)

    @pl.loop(1, ny)
    def _(d):
        t = (y + d) % ny
        scatter(t * nx + x, lambda k: ring_y[t, k], LB + EARLY, late, to_x)

    code = flat[...]
    lane = lax.broadcasted_iota(jnp.int32, code.shape, 1)
    device = lax.broadcasted_iota(jnp.int32, code.shape, 0)
    ours = (code // 256 == row) & (lane >= LB) & (lane < GROUPS * LB)
    value = device * 16 + code % 16
    place = code // 16 % 16
    lines = [jnp.sum(jnp.where(ours & (place == a), value, 0), axis=0, keepdims=True) for a in range(LB)]
    lines += [jnp.zeros_like(lines[0])] * (16 - LB)
    k = lax.broadcasted_iota(jnp.int32, (LANES, LANES), 0)
    g = lax.broadcasted_iota(jnp.int32, (LANES, LANES), 1)
    member = ((k >= g * LB) & (k < g * LB + LB)).astype(F32)
    back_at[...] = hdot(jnp.concatenate(lines, 0).astype(F32), member).astype(jnp.int32)


def build_kernel(
    ny, nx, in_row, in_col, back_at, face_row, face_src, own_val, to_y, to_x, from_y, from_x, face_val, rows_ref, col_at,
    own_at, face_at
):
    n_row = ny * nx
    row = lax.axis_index("row")
    y, x = row // nx, row % nx

    @pl.loop(0, GROUPS)
    def _(g):
        for b in range(LB):
            k = g * LB + b
            own_at[g * LB + in_row[0, 0, k]] = k

    for k in range(LB):
        face_at[face_row[0, 0, k]] = k

    quarter = lax.broadcasted_iota(jnp.int32, (KB, LANES), 1) % KB < HALF
    left = is_left((HALF, LANES))

    def pair(one, two):
        top = jnp.where(left, one, swap(two))
        low = jnp.where(left, swap(one), two)
        return jnp.concatenate([top, low], 0)

    @pl.loop(0, LB)
    def _(a):
        def put(slot, ij, kl):
            lanes = slice(slot * LANES, (slot + 1) * LANES)
            rows_ref[a, :KB, lanes] = jnp.where(quarter, ij, pltpu.roll(kl, HALF, 1)).astype(BF16)
            rows_ref[a, KB:, lanes] = jnp.where(quarter, pltpu.roll(ij, LANES - HALF, 1), kl).astype(BF16)

        own = []
        for g in range(GROUPS):
            k = own_at[g * LB + a]
            col_at[a * SLOTS + g] = in_col[0, 0, k]
            own.append(own_val[k].astype(F32))
        put(0, pair(own[0], own[2]), pair(own[1], own[3]))
        put(1, pair(own[4], own[6]), pair(own[5], own[7]))
        back = []
        for g in range(GROUPS - 1):
            code = back_at[a, g + 1]
            device = code // 16
            col_at[a * SLOTS + GROUPS + g] = device * LB + code % 16
            if (g + 1) * LB <= EARLY:
                slot, t, mine, kept, got = g * LB + a, device // nx, y, to_y, from_y
            else:
                slot, t, mine, kept, got = g * LB - EARLY + a, device % nx, x, to_x, from_x
            back.append(jnp.where(t == mine, kept[mine, slot].astype(F32), got[t, slot].astype(F32)))
        turned = jnp.concatenate([pair(back[0], back[1]), pair(back[2], back[3])], 0).T
        put(2, turned[:KB], turned[KB:])
        turned = jnp.concatenate([pair(back[4], back[5]), pair(back[6], back[6])], 0).T
        k = face_at[a]
        col_at[a * SLOTS + SLOTS - 1] = n_row * LB + face_src[0, 0, k]
        face = face_val[0, 0, k].astype(F32)
        put(3, turned[:KB], jnp.where(is_left((KB, LANES)), turned[KB:], jnp.concatenate([face, face], 1)))


def apply_operator(many, coarse, col_at, rows_ref, own, group, bnd_all, terms, put_row):
    n_row, n_sub = group.shape[0], bnd_all.shape[0]

    def split(values, at, size):
        if coarse:
            terms[pl.ds(at, size)] = values
            return
        for v in range(many):
            hi, mid = two_terms(values[:, v * HALF : (v + 1) * HALF])
            lane = 2 * v * LANES
            terms[pl.ds(at, size), :, lane : lane + LANES] = hi
            terms[pl.ds(at, size), :, lane + LANES : lane + 2 * LANES] = mid

    @pl.loop(0, n_row)
    def _(r):
        split(group[r], r * LB, LB)

    split(own[...], lax.axis_index("row") * LB, LB)

    @pl.loop(0, n_sub)
    def _(t):
        split(bnd_all[t], n_row * LB + t * IFR, IFR)

    together = 3

    @pl.loop(0, LB // together)
    def _(c):
        for i in range(together):
            a = c * together + i
            total = None
            for part in range(2):
                here = range(part * GROUPS, (part + 1) * GROUPS)
                pieces = [terms[col_at[a * SLOTS + t]] for t in here]
                if coarse and part == 0:
                    pieces[0] = jnp.zeros_like(pieces[0])
                stack = jnp.concatenate(pieces, 0)
                lhs = rows_ref[a, :, part * GROUPS * HALF : (part + 1) * GROUPS * HALF]
                product = jnp.dot(lhs, stack, preferred_element_type=F32)
                total = product if total is None else total + product
            blocks = []
            for v in range(many):
                both = add_terms(coarse, total, v)
                blocks.append(both[:KB] + swap(both[KB:]))
            put_row(a, blocks)


def landed_blocks(many, landed, q):
    total = landed[0, q]
    for t in range(1, landed.shape[0]):
        total = total + landed[t, q]
    parts = [total[v * HALF : (v + 1) * HALF] for v in range(many)]
    return [jnp.concatenate([part, swap(part)], 0) for part in parts]


def block_at(a):
    return pl.ds(pl.multiple_of(a * KB, KB), KB)


def first_apply_kernel(col_at, bnd, rows_ref, own, group, bnd_all, landed, basis, image, gram, terms):
    left_block = is_left((KB, LANES))

    def put_row(a, blocks):
        image[block_at(a), :] = jnp.where(left_block, blocks[0], swap(blocks[1]))

    apply_operator(2, False, col_at, rows_ref, own, group, bnd_all, terms, put_row)
    for q in range(IFR):
        one, two = landed_blocks(2, landed, q)
        at = block_at(bnd[0, 0, q])
        image[at, :] = image[at, :] + jnp.where(left_block, one, swap(two))
    both = basis[...]
    left = is_left(both.shape)
    gram[...] = hdot(both.T, jnp.where(left, both, swap(image[...])))


def apply_kernel(
    coarse, col_at, bnd, rows_ref, own, group, bnd_all, landed, current, image_x, basis, image_b, gram, terms, diagonal
):
    left_block = is_left((KB, LANES))

    def put_row(a, blocks):
        at = block_at(a)
        image_b[at, :] = jnp.where(left_block, blocks[0], image_x[at, :])

    apply_operator(1, coarse, col_at, rows_ref, own, group, bnd_all, terms, put_row)
    for q in range(IFR):
        at = block_at(bnd[0, 0, q])
        image_b[at, :] = image_b[at, :] + jnp.where(left_block, landed_blocks(1, landed, q)[0], 0.0)
    y = basis[...]
    turned = y.T
    left = is_left(y.shape)
    if coarse:
        for a in range(LB):
            own_terms = jnp.concatenate(two_terms(pack(y[a * KB : (a + 1) * KB])), 1)
            product = jnp.dot(rows_ref[a, :, :HALF], own_terms, preferred_element_type=F32)
            both = add_terms(False, product, 0)
            diagonal[a * KB : (a + 1) * KB] = both[:KB] + swap(both[KB:])
        twice = jnp.where(left, y + (y - y.astype(BF16).astype(F32)), 0.0)
        gram[0:LANES] = hdot(turned, jnp.where(left, diagonal[...], image_x[...])) + hdot(
            twice.T, jnp.where(left, image_b[...], 0.0)
        )
    else:
        gram[0:LANES] = hdot(turned, image_b[...])
    gram[LANES : 2 * LANES] = hdot(turned, jnp.where(left, image_x[...], swap(current[...])))
    gram[2 * LANES :] = hdot(turned, y)


def eliminate(work, n, full):
    lane = lax.broadcasted_iota(jnp.int32, (n, LANES), 1)
    line = lax.broadcasted_iota(jnp.int32, (n, 1), 0)
    lane1 = lax.broadcasted_iota(jnp.int32, (1, LANES), 1)

    def step(t, pivots):
        j = 2 * t
        k = j + 1
        row0, row1 = work[pl.ds(j, 1), :], work[pl.ds(k, 1), :]
        whole = work[...]

        def entry(row, at):
            return jnp.sum(jnp.where(lane1 == at, row[:, :LANES], 0.0), axis=1, keepdims=True)

        def column(at):
            return jnp.sum(jnp.where(lane == at, whole[:, :LANES], 0.0), axis=1, keepdims=True)

        a, b, c, d = entry(row0, j), entry(row0, k), entry(row1, j), entry(row1, k)
        col0, col1 = column(j), column(k)
        inverse = 1.0 / a
        ratio = b * inverse
        below = row1 - (c * inverse) * row0
        second = d - c * ratio
        unit1 = below * (1.0 / second)
        unit0 = row0 * inverse - ratio * unit1
        moved = whole - (col0 * unit0 + col1 * unit1)
        if full:
            work[...] = jnp.where(line == j, unit0, jnp.where(line == k, unit1, moved))
        else:
            work[...] = jnp.where(line > k, moved, jnp.where(line == k, below, whole))
        return jnp.where(line == j, a, jnp.where(line == k, second, pivots))

    return lax.fori_loop(0, n // 2, step, jnp.zeros((n, 1), F32))


def padded(top):
    return jnp.concatenate([top, jnp.zeros_like(top)], 0)


def identity_right():
    line = lax.broadcasted_iota(jnp.int32, (KB, LANES), 0)
    lane = lax.broadcasted_iota(jnp.int32, (KB, LANES), 1)
    return (lane == line + KB).astype(F32)


def identity_left():
    line = lax.broadcasted_iota(jnp.int32, (KB, LANES), 0)
    lane = lax.broadcasted_iota(jnp.int32, (KB, LANES), 1)
    return (lane == line).astype(F32)


CHUNK = 256


def chunks(body):
    @pl.loop(0, LB * KB // CHUNK)
    def _(c):
        body(pl.ds(pl.multiple_of(c * CHUNK, CHUNK), CHUNK))


def new_basis(ritz, precond, current, image_x, basis, update, at):
    here = current[at, :]
    left = is_left(here.shape)
    residue = jnp.where(left, image_x[at, :], 0.0) - hdot(here, ritz)
    fresh = precond[at, :] * residue
    update[at, :] = fresh
    basis[at, :] = jnp.where(left, fresh, here)


def send_basis(coarse, update, packed, bnd_out, parts, bnd, face_row, face_src, face_val):
    for a in range(LB):
        packed[a] = pack(update[a * KB : (a + 1) * KB, :]).astype(packed.dtype)
    write_messages(1, coarse, packed, bnd_out, parts, bnd, face_row, face_src, face_val)


def first_ritz_kernel(
    bnd, face_row, face_src, gram, face_val, precond, current, image_x, basis, packed, bnd_out, parts, update, work
):
    work[...] = gram[:KB]
    eliminate(work, KB, True)
    left = is_left((KB, LANES))
    ritz = padded(jnp.where(left, swap(work[...]), 0.0))
    chunks(lambda at: new_basis(ritz, precond, current, image_x, basis, update, at))
    send_basis(False, update, packed, bnd_out, parts, bnd, face_row, face_src, face_val)


def combine(total_rows, gram, metric, wide, narrow):
    energy = gram[0:LANES]
    turned = energy.T
    upper = lax.broadcasted_iota(jnp.int32, (LANES, LANES), 0) < KB
    right_half = lax.broadcasted_iota(jnp.int32, (LANES, LANES), 1) >= KB
    crossed = jnp.where(upper, energy, turned)
    wide[:, :LANES] = jnp.where(upper == right_half, crossed, 0.5 * (energy + turned))
    right = gram[LANES : 2 * LANES]
    wide[:, LANES:] = right
    eliminate(wide, LANES, True)
    left_all = is_left((LANES, LANES))
    left = is_left((KB, LANES))
    z = jnp.where(left_all, -wide[:, LANES:], 0.0)
    cross = hdot(right.T, z)
    against = jnp.where(left_all, swap(right), 0.0) + hdot(gram[2 * LANES :], z)
    square = hdot(z.T, against)[:KB]
    lengths = jnp.where(left, metric[...], 0.0) + cross[KB:] + square
    narrow[...] = lengths * (1.0 / total_rows) + identity_right()
    pivots = eliminate(narrow, KB, False)
    root = 1.0 / jnp.sqrt(pivots)
    inverse = padded(jnp.where(left, swap(narrow[...]), 0.0) * root)
    turned = inverse.T
    half = hdot(z, turned)
    energy = jnp.where(left, swap(metric[...]), 0.0) + cross[:KB]
    energy = hdot(hdot(inverse, padded(energy)), turned)
    return turned, jnp.where(left_all, half, swap(half)), energy


def step_kernel(
    total_rows,
    bnd,
    face_row,
    face_src,
    gram,
    metric,
    face_val,
    precond,
    current,
    image_x,
    basis,
    image_b,
    next_metric,
    next_current,
    next_image,
    next_basis,
    packed,
    bnd_out,
    parts,
    update,
    wide,
    narrow,
):
    turned, moves, energy = combine(total_rows, gram, metric, wide, narrow)
    next_metric[...] = identity_left() * total_rows + swap(energy[:KB])
    ritz = energy * (1.0 / total_rows)

    def body(at):
        next_current[at, :] = hdot(current[at, :], turned) + hdot(basis[at, :], moves)
        next_image[at, :] = hdot(image_x[at, :], turned) + hdot(image_b[at, :], moves)
        new_basis(ritz, precond, next_current, next_image, next_basis, update, at)

    chunks(body)
    send_basis(True, update, packed, bnd_out, parts, bnd, face_row, face_src, face_val)


def last_kernel(total_rows, gram, metric, current, basis, modes, search, both, wide, narrow):
    turned, moves, _ = combine(total_rows, gram, metric, wide, narrow)

    def body(at):
        both[at, :] = hdot(current[at, :], turned) + hdot(basis[at, :], moves)

    chunks(body)
    whole = both[...].T
    modes[...] = whole[:KB]
    search[...] = whole[KB:]


def plain(kernel, name, specs, outs, scratch, *args):
    return pl.pallas_call(
        kernel,
        name=name,
        out_shape=outs,
        in_specs=specs,
        out_specs=[VMEM] * len(outs),
        scratch_shapes=scratch,
        compiler_params=pltpu.CompilerParams(vmem_limit_bytes=LIMIT),
    )(*args)


def shape(*dims):
    return jax.ShapeDtypeStruct(dims, F32)


def local(grid, modes, search, precond, in_row, in_col, in_val, bnd_rows, if_row, if_src, if_val):
    n_sub, ny, nx = grid
    n_row = ny * nx
    rows_here = LB * KB
    total_rows = float(rows_here * n_sub * n_row)
    vals = in_val[0, 0]
    own_val = jnp.concatenate([vals[:, :HALF], vals[:, HALF:]], 2)
    faces = (bnd_rows, if_row, if_src)

    def sent(many, kind=F32):
        return [
            jax.ShapeDtypeStruct((LB, many * HALF, LANES), kind),
            jax.ShapeDtypeStruct((IFR, many * HALF, LANES), kind),
            shape(2, n_sub // 2, IFR, many * HALF, LANES),
        ]

    current, shard, bnd, parts, weights = plain(
        start_kernel,
        "start",
        [SMEM] * 3 + [VMEM] * 4,
        [shape(rows_here, LANES), *sent(2), shape(rows_here, LANES)],
        [],
        *faces,
        modes.T,
        search.T,
        precond.reshape(-1, LANES),
        if_val,
    )
    cols = in_col[0]
    codes = cols // LB * 256 + cols % LB * 16 + in_row[0]
    codes = jnp.pad(codes, ((0, 7), (0, LANES - GROUPS * LB)))
    early = own_val[LB : LB + EARLY].reshape(-1, LANES)
    late = own_val[LB + EARLY :].reshape(-1, LANES)
    codes_all, ring_x, ring_y = ring_gather(6, ny, nx, codes, early, late)
    in_early, in_late = EARLY, GROUPS * LB - LB - EARLY

    def blocks(count):
        return jax.ShapeDtypeStruct((count, HALF, LANES), BF16)

    to_y, to_x, back_at = plain(
        functools.partial(select_kernel, ny, nx),
        "select",
        [VMEM] * 4,
        [blocks((ny + 1) * in_early), blocks((nx + 1) * in_late), jax.ShapeDtypeStruct((16, LANES), jnp.int32)],
        [pltpu.VMEM((n_row, LANES), jnp.int32)] * 2
        + [pltpu.SMEM((n_row, LANES), jnp.int32), pltpu.SemaphoreType.DMA],
        codes_all,
        own_val,
        ring_x.reshape(nx, in_early, HALF, LANES),
        ring_y.reshape(ny, in_late, HALF, LANES),
    )
    to_y = to_y.reshape(ny + 1, in_early, HALF, LANES)
    to_x = to_x.reshape(nx + 1, in_late, HALF, LANES)
    group, from_y, from_x, bnd_all, landed = exchange(
        0, ny, nx, [shard.reshape(-1, LANES)], [to_y, to_x], bnd, parts
    )
    block_rows, col_at = pl.pallas_call(
        functools.partial(build_kernel, ny, nx),
        name="build",
        out_shape=[
            jax.ShapeDtypeStruct((LB, 2 * KB, SLOTS * HALF), BF16),
            jax.ShapeDtypeStruct((LB * SLOTS,), jnp.int32),
        ],
        in_specs=[SMEM] * 5 + [VMEM] * 6,
        out_specs=[VMEM, SMEM],
        scratch_shapes=[pltpu.SMEM((GROUPS * LB,), jnp.int32), pltpu.SMEM((LB,), jnp.int32)],
        compiler_params=pltpu.CompilerParams(vmem_limit_bytes=LIMIT),
    )(in_row, in_col, back_at, if_row, if_src, own_val, to_y, to_x, from_y, from_x, if_val)
    blocks_all = n_row * LB + n_sub * IFR
    image_x, gram = plain(
        first_apply_kernel,
        "first_apply",
        [SMEM] * 2 + [VMEM] * 6,
        [shape(rows_here, LANES), shape(LANES, LANES)],
        [pltpu.VMEM((blocks_all, HALF, 4 * LANES), BF16)],
        col_at,
        bnd_rows,
        block_rows,
        shard,
        group.reshape(n_row, LB, 2 * HALF, LANES),
        bnd_all,
        landed,
        current,
    )
    metric = sum_all(1, n_sub, n_row, gram)
    basis, packed, bnd, parts = plain(
        first_ritz_kernel,
        "first_ritz",
        [SMEM] * 3 + [VMEM] * 5,
        [shape(rows_here, LANES), *sent(1)],
        [pltpu.VMEM((rows_here, LANES), F32), pltpu.VMEM((KB, LANES), F32)],
        *faces,
        metric,
        if_val,
        weights,
        current,
        image_x,
    )
    metric = metric[:KB]
    solver = [pltpu.VMEM((rows_here, LANES), F32), pltpu.VMEM((LANES, 2 * LANES), F32), pltpu.VMEM((KB, LANES), F32)]
    for sweep in range(ITERS):
        group, bnd_all, landed = exchange(2 + 2 * sweep, ny, nx, [packed.reshape(-1, LANES)], [], bnd, parts)
        coarse = sweep == ITERS - 1
        image_b, gram = plain(
            functools.partial(apply_kernel, coarse),
            f"apply_{sweep}",
            [SMEM] * 2 + [VMEM] * 8,
            [shape(rows_here, LANES), shape(3 * LANES, LANES)],
            [
                pltpu.VMEM((blocks_all, HALF, LANES if coarse else 2 * LANES), BF16),
                pltpu.VMEM((rows_here, LANES), F32),
            ],
            col_at,
            bnd_rows,
            block_rows,
            packed,
            group.reshape(n_row, LB, HALF, LANES),
            bnd_all,
            landed,
            current,
            image_x,
            basis,
        )
        gram = sum_all(3 + 2 * sweep, n_sub, n_row, gram)
        if sweep < ITERS - 1:
            metric, current, image_x, basis, packed, bnd, parts = plain(
                functools.partial(step_kernel, total_rows),
                "step",
                [SMEM] * 3 + [VMEM] * 8,
                [shape(KB, LANES), shape(rows_here, LANES), shape(rows_here, LANES), shape(rows_here, LANES), *sent(1, BF16)],
                solver,
                *faces,
                gram,
                metric,
                if_val,
                weights,
                current,
                image_x,
                basis,
                image_b,
            )
    modes, search = plain(
        functools.partial(last_kernel, total_rows),
        "last",
        [VMEM] * 4,
        [shape(KB, rows_here), shape(KB, rows_here)],
        solver,
        gram,
        metric,
        current,
        basis,
    )
    return modes.T, search.T


def solution(mesh):
    n_sub, n_row = mesh.shape["sub"], mesh.shape["row"]
    ny = 4 if n_row == 16 else 2
    return jax.shard_map(
        functools.partial(local, (n_sub, ny, n_row // ny)),
        mesh=mesh,
        in_specs=(
            P(("sub", "row"), None),
            P(("sub", "row"), None),
            P(("sub", "row")),
            P("sub", "row", None),
            P("sub", "row", None),
            P("sub", "row", None, None, None),
            P("sub", "row", None),
            P("sub", "row", None),
            P("sub", "row", None),
            P("sub", "row", None, None, None),
        ),
        out_specs=(P(("sub", "row"), None), P(("sub", "row"), None)),
        check_vma=False,
    )
```

```python
import functools

import jax
import jax.numpy as jnp
from jax import lax
from jax.experimental import pallas as pl
from jax.experimental.pallas import tpu as pltpu
from jax.sharding import PartitionSpec as P

KB = 64
LB = 12
IFR = 3
ITERS = 2
GROUPS = 8
HALF = KB // 2
SLOTS = 2 * GROUPS
LANES = 128
MESH = pl.DeviceIdType.MESH
F32, BF16 = jnp.float32, jnp.bfloat16
VMEM = pl.BlockSpec(memory_space=pltpu.VMEM)
SMEM = pl.BlockSpec(memory_space=pltpu.SMEM)
ANY = pl.BlockSpec(memory_space=pl.ANY)
LIMIT = 12 * 1024 * 1024
SMALL = 4 * 1024 * 1024
EARLY = 4 * LB


def hdot(a, b):
    return jnp.dot(a, b, precision=lax.Precision.HIGHEST, preferred_element_type=F32)


def swap(v):
    return pltpu.roll(v, LANES // 2, 1)


def is_left(shape):
    return lax.broadcasted_iota(jnp.int32, shape, 1) < LANES // 2


def pack(block):
    left = is_left((HALF, LANES))
    return jnp.where(left, block[:HALF], swap(block[HALF:]))


def two_terms(v):
    hi = v.astype(BF16)
    return hi, (v - hi.astype(F32)).astype(BF16)


def add_terms(coarse, product, v):
    if coarse:
        return product
    at = 2 * v * LANES
    return product[:, at : at + LANES] + product[:, at + LANES : at + 2 * LANES]


def write_messages(many, coarse, shard, bnd_out, parts, bnd, face_row, face_src, face_val):
    for q in range(IFR):
        bnd_out[q] = shard[bnd[0, 0, q]]
    parts[...] = jnp.zeros_like(parts)
    left = is_left((HALF, LANES))
    products = []
    for k in range(LB):
        block = shard[face_row[0, 0, k]]
        face = face_val[0, 0, k]
        if coarse:
            terms = block
        else:
            terms = jnp.concatenate([t for v in range(many) for t in two_terms(block[v * HALF : (v + 1) * HALF])], 1)
        one, two = (
            lax.dot_general(half, terms, (((0,), (0,)), ((), ())), preferred_element_type=F32)
            for half in (face[:HALF], face[HALF:])
        )
        sums = []
        for v in range(many):
            first, second = add_terms(coarse, one, v), add_terms(coarse, two, v)
            sums.append(
                jnp.where(left, first[:HALF] + swap(second[:HALF]), swap(first[HALF:]) + second[HALF:])
            )
        products.append(jnp.concatenate(sums, 0) if many > 1 else sums[0])
    for k in range(LB):
        source = face_src[0, 0, k]
        target, slot = source // IFR, source % IFR
        core, z = target % 2, target // 2
        parts[core, z, slot] = parts[core, z, slot] + products[k]


def start_kernel(bnd, face_row, face_src, modes, search, precond, face_val, current, *refs):
    first, second, weights = refs[:3], refs[3:6], refs[6]
    current[...] = jnp.concatenate([modes[...], search[...]], 0).T
    for a in range(LB):
        block = current[a * KB : (a + 1) * KB]
        first[0][a] = pack(block)
        second[0][a] = pack(swap(block))
    for c in range(LB * KB // LANES):
        weights[c * LANES : (c + 1) * LANES] = jnp.broadcast_to(precond[c : c + 1], (LANES, LANES)).T
    write_messages(1, False, *first, bnd, face_row, face_src, face_val)
    write_messages(1, False, *second, bnd, face_row, face_src, face_val)


def exchange_steps(greet, count, handing, ny, nx, n_sub, *refs):
    arrays = count + 2 * handing
    shards, bnd, parts = refs[:arrays], refs[arrays], refs[arrays + 1]
    groups, bnd_all, landed = refs[arrays + 2 : 2 * arrays + 2], refs[2 * arrays + 2], refs[2 * arrays + 3]
    theirs, ours, sub_send, sub_recv, row_send, row_recv, ring_send, ring_recv = refs[2 * arrays + 4 :]
    sub, row = lax.axis_index("sub"), lax.axis_index("row")
    y, x = row // nx, row % nx
    nz = n_sub // 2
    z, core = sub // 2, sub % 2
    sibling = z * 2 + 1 - core

    def at(dy, dx):
        return ((y + dy + ny) % ny) * nx + (x + dx + nx) % nx

    def along(d):
        return ((z + d + nz) % nz) * 2 + core

    if greet:
        barrier = pltpu.get_barrier_semaphore()
        for d in range(1, nx):
            pl.semaphore_signal(barrier, inc=1, device_id={"row": at(0, d)}, device_id_type=MESH)
        for d in range(1, ny):
            pl.semaphore_signal(barrier, inc=1, device_id={"row": at(d, 0)}, device_id_type=MESH)
        for d in range(1, nz):
            pl.semaphore_signal(barrier, inc=1, device_id={"sub": along(d)}, device_id_type=MESH)
        pl.semaphore_signal(barrier, inc=1, device_id={"sub": sibling}, device_id_type=MESH)
        pl.semaphore_wait(barrier, nx - 1 + ny - 1 + nz)

    def to_sub(src, dst, kind, d, target):
        return pltpu.make_async_remote_copy(
            src_ref=src,
            dst_ref=dst,
            send_sem=sub_send.at[kind, d],
            recv_sem=sub_recv.at[kind, d],
            device_id={"sub": target},
            device_id_type=MESH,
        )

    def landed_at(ref, sem):
        pltpu.make_async_copy(ref, ref, sem).wait()

    def hop(i, half, holder, src, to, sem):
        size = shards[i].shape[0] // 2
        return pltpu.make_async_remote_copy(
            src_ref=src,
            dst_ref=groups[i].at[holder, pl.ds(half * size, size)],
            send_sem=row_send.at[i, half, sem],
            recv_sem=row_recv.at[i, half, sem],
            device_id={"row": to},
            device_id_type=MESH,
        )

    def half_of(i, half, holder=None):
        size = shards[i].shape[0] // 2
        part = pl.ds(half * size, size)
        return shards[i].at[part] if holder is None else groups[i].at[holder, part]

    counts = ((nx, ny), (ny, nx))

    def place(half, first, second):
        return at(second, first) if half == 0 else at(first, second)

    sends = []

    def send(copy):
        copy.start()
        sends.append(copy)

    send(to_sub(parts.at[1 - core], theirs, 3, 0, sibling))
    for i in range(count):
        for half in range(2):
            n1, n2 = counts[half]
            for first in range(1, n1):
                send(hop(i, half, row, half_of(i, half), place(half, first, 0), first * n2))
        if i == 0:
            for d in range(1, nz):
                send(to_sub(bnd, bnd_all.at[sub], 0, d, along(d)))
            send(to_sub(bnd, bnd_all.at[sub], 1, 0, sibling))
        for half in range(2):
            n1, n2 = counts[half]
            for second in range(1, n2):
                send(hop(i, half, row, half_of(i, half), place(half, 0, second), second))

    for axis in range(2 * handing):
        mine, n = (y, x)[axis], (ny, nx)[axis]
        for d in range(1, n):
            t = (mine + d) % n
            send(
                pltpu.make_async_remote_copy(
                    src_ref=shards[count + axis].at[t],
                    dst_ref=groups[count + axis].at[mine],
                    send_sem=ring_send.at[axis, d],
                    recv_sem=ring_recv.at[axis, d],
                    device_id={"row": (t * nx + x, y * nx + t)[axis]},
                    device_id_type=MESH,
                )
            )

    yield
    landed_at(theirs, sub_recv.at[3, 0])
    ours[...] = theirs[...] + parts[core]
    for d in range(1, nz):
        send(to_sub(ours.at[(z + d) % nz], landed.at[z], 2, d, along(d)))
    landed[z] = ours[z]

    for i in range(count):
        for first in range(1, max(nx, ny)):
            for half in range(2):
                n1, n2 = counts[half]
                if first >= n1:
                    continue
                holder = place(half, -first, 0)
                landed_at(half_of(i, half, holder), row_recv.at[i, half, first * n2])
                for second in range(1, n2):
                    send(hop(i, half, holder, half_of(i, half, holder), place(half, 0, second), first * n2 + second))
        if i == 0:
            for d in range(1, nz):
                here = bnd_all.at[along(-d)]
                landed_at(here, sub_recv.at[0, d])
                send(to_sub(here, here, 1, d, sibling))
    yield
    for d in range(1, nz):
        landed_at(landed.at[(z + nz - d) % nz], sub_recv.at[2, d])
    for d in range(nz):
        landed_at(bnd_all.at[((z + nz - d) % nz) * 2 + 1 - core], sub_recv.at[1, d])
    for i in range(count):
        for half in range(2):
            n1, n2 = counts[half]
            for first in range(n1):
                for second in range(1, n2):
                    landed_at(half_of(i, half, place(half, -first, -second)), row_recv.at[i, half, first * n2 + second])
    for axis in range(2 * handing):
        mine, n = (y, x)[axis], (ny, nx)[axis]
        for d in range(1, n):
            landed_at(groups[count + axis].at[(mine + n - d) % n], ring_recv.at[axis, d])
    for copy in sends:
        copy.wait_send()


def exchange_kernel(*args):
    for _ in exchange_steps(True, *args):
        pass


def exchange_scratch(count, ny, nx, parts):
    most, n_row = max(parts.shape[1], 2), ny * nx
    return [
        pltpu.VMEM(parts.shape[1:], F32),
        pltpu.VMEM(parts.shape[1:], F32),
        pltpu.SemaphoreType.DMA((4, most)),
        pltpu.SemaphoreType.DMA((4, most)),
        pltpu.SemaphoreType.DMA((count, 2, n_row)),
        pltpu.SemaphoreType.DMA((count, 2, n_row)),
        pltpu.SemaphoreType.DMA((2, max(nx, ny))),
        pltpu.SemaphoreType.DMA((2, max(nx, ny))),
    ]


def exchange(collective_id, ny, nx, shards, handed, bnd, parts):
    count, n_row = len(shards), ny * nx
    nz = parts.shape[1]
    n_sub = 2 * nz
    gathered = [jax.ShapeDtypeStruct((n_row, *a.shape), a.dtype) for a in shards]
    gathered += [jax.ShapeDtypeStruct((n, *a.shape[1:]), a.dtype) for n, a in zip((ny, nx), handed)]
    return pl.pallas_call(
        functools.partial(exchange_kernel, count, bool(handed), ny, nx, n_sub),
        name=f"exchange_{collective_id}",
        out_shape=gathered
        + [jax.ShapeDtypeStruct((n_sub, *bnd.shape), bnd.dtype), jax.ShapeDtypeStruct(parts.shape[1:], F32)],
        in_specs=[VMEM] * (len(gathered) + 2),
        out_specs=[VMEM] * (len(gathered) + 2),
        scratch_shapes=exchange_scratch(count, ny, nx, parts),
        compiler_params=pltpu.CompilerParams(
            collective_id=collective_id, has_side_effects=True, vmem_limit_bytes=SMALL
        ),
    )(*shards, *handed, bnd, parts)


def rings_kernel(ny, nx, codes, early, late, codes_all, ring_x, ring_y, send, recv):
    row = lax.axis_index("row")
    y, x = row // nx, row % nx
    n_row = ny * nx
    barrier = pltpu.get_barrier_semaphore()
    for d in range(1, n_row):
        pl.semaphore_signal(barrier, inc=1, device_id={"row": (row + d) % n_row}, device_id_type=MESH)
    pl.semaphore_wait(barrier, n_row - 1)
    rings = (
        (nx, x, lambda t: y * nx + t, early, ring_x),
        (ny, y, lambda t: t * nx + x, late, ring_y),
        (n_row, row, lambda t: t, codes, codes_all),
    )
    sends = []
    order = [(2, d) for d in range(1, n_row)]
    for d in range(1, max(nx, ny)):
        order += [(i, (d, rings[i][0] - d)[i]) for i in range(2) if d < rings[i][0]]
    for i, d in order:
        n, mine, name, src, dst = rings[i]
        copy = pltpu.make_async_remote_copy(
            src_ref=src,
            dst_ref=dst.at[mine],
            send_sem=send.at[i, d],
            recv_sem=recv.at[i, d],
            device_id={"row": name((mine + d) % n)},
            device_id_type=MESH,
        )
        copy.start()
        sends.append(copy)
    codes_all[row] = codes[...]
    for i, (n, mine, _, _, dst) in enumerate(rings):
        for d in range(1, n):
            here = dst.at[(mine + n - d) % n]
            pltpu.make_async_copy(here, here, recv.at[i, d]).wait()
    for copy in sends:
        copy.wait_send()


def ring_gather(collective_id, ny, nx, codes, early, late):
    return pl.pallas_call(
        functools.partial(rings_kernel, ny, nx),
        name=f"rings_{collective_id}",
        out_shape=[
            jax.ShapeDtypeStruct((n, *a.shape), a.dtype) for n, a in ((ny * nx, codes), (nx, early), (ny, late))
        ],
        in_specs=[VMEM] * 3,
        out_specs=[VMEM] * 3,
        scratch_shapes=[pltpu.SemaphoreType.DMA((3, ny * nx))] * 2,
        compiler_params=pltpu.CompilerParams(
            collective_id=collective_id, has_side_effects=True, vmem_limit_bytes=SMALL
        ),
    )(codes, early, late)


def sum_steps(n_sub, n_row, parts, out, by_row, by_sub, own_sem, send, recv):
    sub, row = lax.axis_index("sub"), lax.axis_index("row")
    barrier = pltpu.get_barrier_semaphore()

    @pl.loop(1, n_row)
    def _(d):
        pl.semaphore_signal(barrier, inc=1, device_id={"row": (row + d) % n_row}, device_id_type=MESH)

    @pl.loop(1, n_sub)
    def _(d):
        pl.semaphore_signal(barrier, inc=1, device_id={"sub": (sub + d) % n_sub}, device_id_type=MESH)

    pl.semaphore_wait(barrier, n_row - 1 + n_sub - 1)

    def phase(index, axis, mine, n, source, target):
        def to(d):
            t = (mine + d) % n
            return pltpu.make_async_remote_copy(
                src_ref=source(t),
                dst_ref=target(mine),
                send_sem=send.at[index, d],
                recv_sem=recv.at[index, d],
                device_id={axis: t},
                device_id_type=MESH,
            )

        own = pltpu.make_async_copy(source(mine), target(mine), own_sem.at[index])

        @pl.loop(1, n)
        def _(d):
            to(d).start()

        own.start()
        yield

        @pl.loop(1, n)
        def _(d):
            here = target((mine + n - d) % n)
            pltpu.make_async_copy(here, here, recv.at[index, d]).wait()
            to(d).wait_send()

        own.wait()

    def summed(buffer, n):
        total = buffer[0]
        for t in range(1, n):
            total = total + buffer[t]
        return total

    yield from phase(0, "row", row, n_row, lambda t: parts.at[t], lambda t: by_row.at[t])
    by_row[n_row] = summed(by_row, n_row)
    yield from phase(1, "sub", sub, n_sub, lambda t: by_row.at[n_row], lambda t: by_sub.at[t])
    by_sub[n_sub] = summed(by_sub, n_sub)
    yield from phase(2, "row", row, n_row, lambda t: by_sub.at[n_sub], lambda t: out.at[t])


def sum_kernel(*args):
    for _ in sum_steps(*args):
        pass


def sum_scratch(n_sub, n_row, rows):
    most = max(n_sub, n_row)
    return [
        pltpu.VMEM((n_row + 1, rows, LANES), F32),
        pltpu.VMEM((n_sub + 1, rows, LANES), F32),
        pltpu.SemaphoreType.DMA((3,)),
        pltpu.SemaphoreType.DMA((3, most)),
        pltpu.SemaphoreType.DMA((3, most)),
    ]


def sum_all(collective_id, n_sub, n_row, part):
    rows = part.shape[0] // n_row
    shape = (n_row, rows, LANES)
    total = pl.pallas_call(
        functools.partial(sum_kernel, n_sub, n_row),
        name=f"sum_{collective_id}",
        out_shape=jax.ShapeDtypeStruct(shape, F32),
        in_specs=[VMEM],
        out_specs=VMEM,
        scratch_shapes=sum_scratch(n_sub, n_row, rows),
        compiler_params=pltpu.CompilerParams(
            collective_id=collective_id, has_side_effects=True, vmem_limit_bytes=SMALL
        ),
    )(part.reshape(shape))
    return total.reshape(part.shape)


def sum_beside_exchange_kernel(ny, nx, n_sub, part, shard, bnd, parts, total, group, bnd_all, landed, *scratch):
    summing = sum_steps(n_sub, ny * nx, part, total, *scratch[:5])
    moving = exchange_steps(
        False, 1, False, ny, nx, n_sub, shard, bnd, parts, group, bnd_all, landed, *scratch[5:]
    )
    for _ in range(3):
        next(summing)
        next(moving, None)
    for _ in summing:
        pass


def sum_beside_exchange(collective_id, ny, nx, part, shard, bnd, parts):
    n_row = ny * nx
    n_sub = 2 * parts.shape[1]
    rows = part.shape[0] // n_row
    total, *moved = pl.pallas_call(
        functools.partial(sum_beside_exchange_kernel, ny, nx, n_sub),
        name=f"sum_beside_exchange_{collective_id}",
        out_shape=[
            shape(n_row, rows, LANES),
            shape(n_row, *shard.shape),
            shape(n_sub, *bnd.shape),
            shape(*parts.shape[1:]),
        ],
        in_specs=[VMEM] * 4,
        out_specs=[VMEM] * 4,
        scratch_shapes=sum_scratch(n_sub, n_row, rows) + exchange_scratch(1, ny, nx, parts),
        compiler_params=pltpu.CompilerParams(
            collective_id=collective_id, has_side_effects=True, vmem_limit_bytes=SMALL
        ),
    )(part.reshape(n_row, rows, LANES), shard, bnd, parts)
    return total.reshape(part.shape), *moved


def select_kernel(ny, nx, codes, own_val, ring_x, ring_y, to_y, to_x, back_at, flat, goes, goes_at, sem):
    row = lax.axis_index("row")
    y, x = row // nx, row % nx
    late = LB * GROUPS - LB - EARLY
    flat[...] = codes[:, 0, :]
    value = flat[...]
    owner, within = value // 256, value // 16 % 16
    at = lax.broadcasted_iota(jnp.int32, value.shape, 1)
    member = jnp.zeros_like(at)
    for g in range(1, GROUPS):
        member = member + jnp.where(at >= g * LB, LB, 0)
    by_x = jnp.where(owner % nx == x, owner // nx, ny) * EARLY + member - LB + within
    by_y = jnp.where(owner // nx == y, owner % nx, nx) * late + member - LB - EARLY + within
    goes[...] = jnp.where(at < LB + EARLY, by_x, by_y)
    copy = pltpu.make_async_copy(goes, goes_at, sem)
    copy.start()
    copy.wait()

    def scatter(device, source, start, size, out):
        @pl.loop(0, size // LB)
        def _(g):
            for b in range(LB):
                k = g * LB + b
                out[goes_at[device, start + k]] = source(k)

    scatter(row, lambda k: own_val[LB + k], LB, EARLY, to_y)
    scatter(row, lambda k: own_val[LB + EARLY + k], LB + EARLY, late, to_x)

    @pl.loop(1, nx)
    def _(d):
        t = (x + d) % nx
        scatter(y * nx + t, lambda k: ring_x[t, k], LB, EARLY, to_y)

    @pl.loop(1, ny)
    def _(d):
        t = (y + d) % ny
        scatter(t * nx + x, lambda k: ring_y[t, k], LB + EARLY, late, to_x)

    code = flat[...]
    lane = lax.broadcasted_iota(jnp.int32, code.shape, 1)
    device = lax.broadcasted_iota(jnp.int32, code.shape, 0)
    ours = (code // 256 == row) & (lane >= LB) & (lane < GROUPS * LB)
    value = device * 16 + code % 16
    place = code // 16 % 16
    lines = [jnp.sum(jnp.where(ours & (place == a), value, 0), axis=0, keepdims=True) for a in range(LB)]
    lines += [jnp.zeros_like(lines[0])] * (16 - LB)
    k = lax.broadcasted_iota(jnp.int32, (LANES, LANES), 0)
    g = lax.broadcasted_iota(jnp.int32, (LANES, LANES), 1)
    member = ((k >= g * LB) & (k < g * LB + LB)).astype(F32)
    back_at[...] = hdot(jnp.concatenate(lines, 0).astype(F32), member).astype(jnp.int32)


def build_kernel(
    ny, nx, in_row, in_col, back_at, face_row, face_src, own_val, to_y, to_x, from_y, from_x, face_val, rows_ref, col_at,
    own_at, face_at
):
    n_row = ny * nx
    row = lax.axis_index("row")
    y, x = row // nx, row % nx

    @pl.loop(0, GROUPS)
    def _(g):
        for b in range(LB):
            k = g * LB + b
            own_at[g * LB + in_row[0, 0, k]] = k

    for k in range(LB):
        face_at[face_row[0, 0, k]] = k

    quarter = lax.broadcasted_iota(jnp.int32, (KB, LANES), 1) % KB < HALF
    left = is_left((HALF, LANES))

    def pair(one, two):
        top = jnp.where(left, one, swap(two))
        low = jnp.where(left, swap(one), two)
        return jnp.concatenate([top, low], 0)

    @pl.loop(0, LB)
    def _(a):
        def put(slot, ij, kl):
            lanes = slice(slot * LANES, (slot + 1) * LANES)
            rows_ref[a, :KB, lanes] = jnp.where(quarter, ij, pltpu.roll(kl, HALF, 1)).astype(BF16)
            rows_ref[a, KB:, lanes] = jnp.where(quarter, pltpu.roll(ij, LANES - HALF, 1), kl).astype(BF16)

        own = []
        for g in range(GROUPS):
            k = own_at[g * LB + a]
            col_at[a * SLOTS + g] = in_col[0, 0, k]
            own.append(own_val[k].astype(F32))
        put(0, pair(own[0], own[2]), pair(own[1], own[3]))
        put(1, pair(own[4], own[6]), pair(own[5], own[7]))
        back = []
        for g in range(GROUPS - 1):
            code = back_at[a, g + 1]
            device = code // 16
            col_at[a * SLOTS + GROUPS + g] = device * LB + code % 16
            if (g + 1) * LB <= EARLY:
                slot, t, mine, kept, got = g * LB + a, device // nx, y, to_y, from_y
            else:
                slot, t, mine, kept, got = g * LB - EARLY + a, device % nx, x, to_x, from_x
            back.append(jnp.where(t == mine, kept[mine, slot].astype(F32), got[t, slot].astype(F32)))
        turned = jnp.concatenate([pair(back[0], back[1]), pair(back[2], back[3])], 0).T
        put(2, turned[:KB], turned[KB:])
        turned = jnp.concatenate([pair(back[4], back[5]), pair(back[6], back[6])], 0).T
        k = face_at[a]
        col_at[a * SLOTS + SLOTS - 1] = n_row * LB + face_src[0, 0, k]
        face = face_val[0, 0, k].astype(F32)
        put(3, turned[:KB], jnp.where(is_left((KB, LANES)), turned[KB:], jnp.concatenate([face, face], 1)))


def apply_operator(many, coarse, col_at, rows_ref, own, group, bnd_all, terms, put_row):
    n_row, n_sub = group.shape[0], bnd_all.shape[0]

    def split(values, at, size):
        if coarse:
            terms[pl.ds(at, size)] = values
            return
        for v in range(many):
            hi, mid = two_terms(values[:, v * HALF : (v + 1) * HALF])
            lane = 2 * v * LANES
            terms[pl.ds(at, size), :, lane : lane + LANES] = hi
            terms[pl.ds(at, size), :, lane + LANES : lane + 2 * LANES] = mid

    @pl.loop(0, n_row)
    def _(r):
        split(group[r], r * LB, LB)

    split(own[...], lax.axis_index("row") * LB, LB)

    @pl.loop(0, n_sub)
    def _(t):
        split(bnd_all[t], n_row * LB + t * IFR, IFR)

    together = 3

    @pl.loop(0, LB // together)
    def _(c):
        for i in range(together):
            a = c * together + i
            total = None
            for part in range(2):
                here = range(part * GROUPS, (part + 1) * GROUPS)
                pieces = [terms[col_at[a * SLOTS + t]] for t in here]
                if coarse and part == 0:
                    pieces[0] = jnp.zeros_like(pieces[0])
                stack = jnp.concatenate(pieces, 0)
                lhs = rows_ref[a, :, part * GROUPS * HALF : (part + 1) * GROUPS * HALF]
                product = jnp.dot(lhs, stack, preferred_element_type=F32)
                total = product if total is None else total + product
            blocks = []
            for v in range(many):
                both = add_terms(coarse, total, v)
                blocks.append(both[:KB] + swap(both[KB:]))
            put_row(a, blocks)


def landed_blocks(many, landed, q):
    total = landed[0, q]
    for t in range(1, landed.shape[0]):
        total = total + landed[t, q]
    parts = [total[v * HALF : (v + 1) * HALF] for v in range(many)]
    return [jnp.concatenate([part, swap(part)], 0) for part in parts]


def block_at(a):
    return pl.ds(pl.multiple_of(a * KB, KB), KB)


def first_apply_kernel(col_at, bnd, rows_ref, own, group, bnd_all, landed, basis, image, gram, terms):
    left_block = is_left((KB, LANES))

    def put_row(a, blocks):
        image[block_at(a), :] = jnp.where(left_block, blocks[0], 0.0)

    apply_operator(1, False, col_at, rows_ref, own, group, bnd_all, terms, put_row)
    for q in range(IFR):
        at = block_at(bnd[0, 0, q])
        image[at, :] = image[at, :] + jnp.where(left_block, landed_blocks(1, landed, q)[0], 0.0)
    both = basis[...]
    left = is_left(both.shape)
    gram[...] = hdot(both.T, jnp.where(left, both, swap(image[...])))


def apply_kernel(coarse, col_at, bnd, rows_ref, own, group, bnd_all, landed, *refs):
    *search, current, image_x, basis, image_b, gram, terms, diagonal = refs
    left_block = is_left((KB, LANES))
    source = image_x
    if search:
        source = image_b

        def put_search(a, blocks):
            image_b[block_at(a), :] = swap(blocks[0])

        apply_operator(1, False, col_at, rows_ref, *search[:3], terms, put_search)
        for q in range(IFR):
            at = block_at(bnd[0, 0, q])
            image_b[at, :] = image_b[at, :] + jnp.where(left_block, 0.0, swap(landed_blocks(1, search[3], q)[0]))

    def put_row(a, blocks):
        at = block_at(a)
        image_b[at, :] = jnp.where(left_block, blocks[0], source[at, :])

    apply_operator(1, coarse, col_at, rows_ref, own, group, bnd_all, terms, put_row)
    for q in range(IFR):
        at = block_at(bnd[0, 0, q])
        image_b[at, :] = image_b[at, :] + jnp.where(left_block, landed_blocks(1, landed, q)[0], 0.0)
    y = basis[...]
    turned = y.T
    left = is_left(y.shape)
    if coarse:
        for a in range(LB):
            own_terms = jnp.concatenate(two_terms(pack(y[a * KB : (a + 1) * KB])), 1)
            product = jnp.dot(rows_ref[a, :, :HALF], own_terms, preferred_element_type=F32)
            both = add_terms(False, product, 0)
            diagonal[a * KB : (a + 1) * KB] = both[:KB] + swap(both[KB:])
        twice = jnp.where(left, y + (y - y.astype(BF16).astype(F32)), 0.0)
        gram[0:LANES] = hdot(turned, jnp.where(left, diagonal[...], image_x[...])) + hdot(
            twice.T, jnp.where(left, image_b[...], 0.0)
        )
    else:
        gram[0:LANES] = hdot(turned, image_b[...])
    gram[LANES : 2 * LANES] = hdot(turned, jnp.where(left, image_x[...], swap(current[...])))
    gram[2 * LANES :] = hdot(turned, y)


def eliminate(work, n, full):
    lane = lax.broadcasted_iota(jnp.int32, (n, LANES), 1)
    line = lax.broadcasted_iota(jnp.int32, (n, 1), 0)
    lane1 = lax.broadcasted_iota(jnp.int32, (1, LANES), 1)

    def step(t, pivots):
        j = 2 * t
        k = j + 1
        row0, row1 = work[pl.ds(j, 1), :], work[pl.ds(k, 1), :]
        whole = work[...]

        def entry(row, at):
            return jnp.sum(jnp.where(lane1 == at, row[:, :LANES], 0.0), axis=1, keepdims=True)

        def column(at):
            return jnp.sum(jnp.where(lane == at, whole[:, :LANES], 0.0), axis=1, keepdims=True)

        a, b, c, d = entry(row0, j), entry(row0, k), entry(row1, j), entry(row1, k)
        col0, col1 = column(j), column(k)
        inverse = 1.0 / a
        ratio = b * inverse
        below = row1 - (c * inverse) * row0
        second = d - c * ratio
        unit1 = below * (1.0 / second)
        unit0 = row0 * inverse - ratio * unit1
        moved = whole - (col0 * unit0 + col1 * unit1)
        if full:
            work[...] = jnp.where(line == j, unit0, jnp.where(line == k, unit1, moved))
        else:
            work[...] = jnp.where(line > k, moved, jnp.where(line == k, below, whole))
        return jnp.where(line == j, a, jnp.where(line == k, second, pivots))

    return lax.fori_loop(0, n // 2, step, jnp.zeros((n, 1), F32))


def padded(top):
    return jnp.concatenate([top, jnp.zeros_like(top)], 0)


def identity_right():
    line = lax.broadcasted_iota(jnp.int32, (KB, LANES), 0)
    lane = lax.broadcasted_iota(jnp.int32, (KB, LANES), 1)
    return (lane == line + KB).astype(F32)


def identity_left():
    line = lax.broadcasted_iota(jnp.int32, (KB, LANES), 0)
    lane = lax.broadcasted_iota(jnp.int32, (KB, LANES), 1)
    return (lane == line).astype(F32)


CHUNK = 256


def chunks(body):
    @pl.loop(0, LB * KB // CHUNK)
    def _(c):
        body(pl.ds(pl.multiple_of(c * CHUNK, CHUNK), CHUNK))


def new_basis(ritz, precond, current, image_x, basis, update, at):
    here = current[at, :]
    left = is_left(here.shape)
    residue = jnp.where(left, image_x[at, :], 0.0) - hdot(here, ritz)
    fresh = precond[at, :] * residue
    update[at, :] = fresh
    basis[at, :] = jnp.where(left, fresh, here)


def send_basis(coarse, update, packed, bnd_out, parts, bnd, face_row, face_src, face_val):
    for a in range(LB):
        packed[a] = pack(update[a * KB : (a + 1) * KB, :]).astype(packed.dtype)
    write_messages(1, coarse, packed, bnd_out, parts, bnd, face_row, face_src, face_val)


def first_ritz_kernel(
    bnd, face_row, face_src, gram, face_val, precond, current, image_x, basis, packed, bnd_out, parts, update, work
):
    work[...] = gram[:KB]
    eliminate(work, KB, True)
    left = is_left((KB, LANES))
    ritz = padded(jnp.where(left, swap(work[...]), 0.0))
    chunks(lambda at: new_basis(ritz, precond, current, image_x, basis, update, at))
    send_basis(False, update, packed, bnd_out, parts, bnd, face_row, face_src, face_val)


def combine(total_rows, gram, metric, wide, narrow):
    energy = gram[0:LANES]
    turned = energy.T
    upper = lax.broadcasted_iota(jnp.int32, (LANES, LANES), 0) < KB
    right_half = lax.broadcasted_iota(jnp.int32, (LANES, LANES), 1) >= KB
    crossed = jnp.where(upper, energy, turned)
    wide[:, :LANES] = jnp.where(upper == right_half, crossed, 0.5 * (energy + turned))
    right = gram[LANES : 2 * LANES]
    wide[:, LANES:] = right
    eliminate(wide, LANES, True)
    left_all = is_left((LANES, LANES))
    left = is_left((KB, LANES))
    z = jnp.where(left_all, -wide[:, LANES:], 0.0)
    cross = hdot(right.T, z)
    against = jnp.where(left_all, swap(right), 0.0) + hdot(gram[2 * LANES :], z)
    square = hdot(z.T, against)[:KB]
    lengths = jnp.where(left, metric[...], 0.0) + cross[KB:] + square
    narrow[...] = lengths * (1.0 / total_rows) + identity_right()
    pivots = eliminate(narrow, KB, False)
    root = 1.0 / jnp.sqrt(pivots)
    inverse = padded(jnp.where(left, swap(narrow[...]), 0.0) * root)
    turned = inverse.T
    half = hdot(z, turned)
    energy = jnp.where(left, swap(metric[...]), 0.0) + cross[:KB]
    energy = hdot(hdot(inverse, padded(energy)), turned)
    return turned, jnp.where(left_all, half, swap(half)), energy


def step_kernel(
    total_rows,
    bnd,
    face_row,
    face_src,
    gram,
    metric,
    face_val,
    precond,
    current,
    image_x,
    basis,
    image_b,
    next_metric,
    next_current,
    next_image,
    next_basis,
    packed,
    bnd_out,
    parts,
    update,
    wide,
    narrow,
):
    turned, moves, energy = combine(total_rows, gram, metric, wide, narrow)
    next_metric[...] = identity_left() * total_rows + swap(energy[:KB])
    ritz = energy * (1.0 / total_rows)

    def body(at):
        next_current[at, :] = hdot(current[at, :], turned) + hdot(basis[at, :], moves)
        next_image[at, :] = hdot(image_x[at, :], turned) + hdot(image_b[at, :], moves)
        new_basis(ritz, precond, next_current, next_image, next_basis, update, at)

    chunks(body)
    send_basis(True, update, packed, bnd_out, parts, bnd, face_row, face_src, face_val)


def last_kernel(total_rows, gram, metric, current, basis, modes, search, both, wide, narrow):
    turned, moves, _ = combine(total_rows, gram, metric, wide, narrow)

    def body(at):
        both[at, :] = hdot(current[at, :], turned) + hdot(basis[at, :], moves)

    chunks(body)
    whole = both[...].T
    modes[...] = whole[:KB]
    search[...] = whole[KB:]


def plain(kernel, name, specs, outs, scratch, *args):
    return pl.pallas_call(
        kernel,
        name=name,
        out_shape=outs,
        in_specs=specs,
        out_specs=[VMEM] * len(outs),
        scratch_shapes=scratch,
        compiler_params=pltpu.CompilerParams(vmem_limit_bytes=LIMIT),
    )(*args)


def shape(*dims):
    return jax.ShapeDtypeStruct(dims, F32)


def local(grid, modes, search, precond, in_row, in_col, in_val, bnd_rows, if_row, if_src, if_val):
    n_sub, ny, nx = grid
    n_row = ny * nx
    rows_here = LB * KB
    total_rows = float(rows_here * n_sub * n_row)
    vals = in_val[0, 0]
    own_val = jnp.concatenate([vals[:, :HALF], vals[:, HALF:]], 2)
    faces = (bnd_rows, if_row, if_src)

    def sent(many, kind=F32):
        return [
            jax.ShapeDtypeStruct((LB, many * HALF, LANES), kind),
            jax.ShapeDtypeStruct((IFR, many * HALF, LANES), kind),
            shape(2, n_sub // 2, IFR, many * HALF, LANES),
        ]

    current, shard, bnd, parts, shard_p, bnd_p, parts_p, weights = plain(
        start_kernel,
        "start",
        [SMEM] * 3 + [VMEM] * 4,
        [shape(rows_here, LANES), *sent(1), *sent(1), shape(rows_here, LANES)],
        [],
        *faces,
        modes.T,
        search.T,
        precond.reshape(-1, LANES),
        if_val,
    )
    cols = in_col[0]
    codes = cols // LB * 256 + cols % LB * 16 + in_row[0]
    codes = jnp.pad(codes, ((0, 7), (0, LANES - GROUPS * LB)))
    early = own_val[LB : LB + EARLY].reshape(-1, LANES)
    late = own_val[LB + EARLY :].reshape(-1, LANES)
    codes_all, ring_x, ring_y = ring_gather(6, ny, nx, codes, early, late)
    in_early, in_late = EARLY, GROUPS * LB - LB - EARLY

    def blocks(count):
        return jax.ShapeDtypeStruct((count, HALF, LANES), BF16)

    to_y, to_x, back_at = plain(
        functools.partial(select_kernel, ny, nx),
        "select",
        [VMEM] * 4,
        [blocks((ny + 1) * in_early), blocks((nx + 1) * in_late), jax.ShapeDtypeStruct((16, LANES), jnp.int32)],
        [pltpu.VMEM((n_row, LANES), jnp.int32)] * 2
        + [pltpu.SMEM((n_row, LANES), jnp.int32), pltpu.SemaphoreType.DMA],
        codes_all,
        own_val,
        ring_x.reshape(nx, in_early, HALF, LANES),
        ring_y.reshape(ny, in_late, HALF, LANES),
    )
    to_y = to_y.reshape(ny + 1, in_early, HALF, LANES)
    to_x = to_x.reshape(nx + 1, in_late, HALF, LANES)
    group, from_y, from_x, bnd_all, landed = exchange(
        0, ny, nx, [shard.reshape(-1, LANES)], [to_y, to_x], bnd, parts
    )
    block_rows, col_at = pl.pallas_call(
        functools.partial(build_kernel, ny, nx),
        name="build",
        out_shape=[
            jax.ShapeDtypeStruct((LB, 2 * KB, SLOTS * HALF), BF16),
            jax.ShapeDtypeStruct((LB * SLOTS,), jnp.int32),
        ],
        in_specs=[SMEM] * 5 + [VMEM] * 6,
        out_specs=[VMEM, SMEM],
        scratch_shapes=[pltpu.SMEM((GROUPS * LB,), jnp.int32), pltpu.SMEM((LB,), jnp.int32)],
        compiler_params=pltpu.CompilerParams(vmem_limit_bytes=LIMIT),
    )(in_row, in_col, back_at, if_row, if_src, own_val, to_y, to_x, from_y, from_x, if_val)
    blocks_all = n_row * LB + n_sub * IFR
    image_x, gram = plain(
        first_apply_kernel,
        "first_apply",
        [SMEM] * 2 + [VMEM] * 6,
        [shape(rows_here, LANES), shape(LANES, LANES)],
        [pltpu.VMEM((blocks_all, HALF, 2 * LANES), BF16)],
        col_at,
        bnd_rows,
        block_rows,
        shard,
        group.reshape(n_row, LB, HALF, LANES),
        bnd_all,
        landed,
        current,
    )
    metric, group_p, bnd_p, landed_p = sum_beside_exchange(1, ny, nx, gram, shard_p.reshape(-1, LANES), bnd_p, parts_p)
    basis, packed, bnd, parts = plain(
        first_ritz_kernel,
        "first_ritz",
        [SMEM] * 3 + [VMEM] * 5,
        [shape(rows_here, LANES), *sent(1)],
        [pltpu.VMEM((rows_here, LANES), F32), pltpu.VMEM((KB, LANES), F32)],
        *faces,
        metric,
        if_val,
        weights,
        current,
        image_x,
    )
    metric = metric[:KB]
    solver = [pltpu.VMEM((rows_here, LANES), F32), pltpu.VMEM((LANES, 2 * LANES), F32), pltpu.VMEM((KB, LANES), F32)]
    for sweep in range(ITERS):
        group, bnd_all, landed = exchange(2 + 2 * sweep, ny, nx, [packed.reshape(-1, LANES)], [], bnd, parts)
        coarse = sweep == ITERS - 1
        image_b, gram = plain(
            functools.partial(apply_kernel, coarse),
            f"apply_{sweep}",
            [SMEM] * 2 + [VMEM] * (12 if sweep == 0 else 8),
            [shape(rows_here, LANES), shape(3 * LANES, LANES)],
            [
                pltpu.VMEM((blocks_all, HALF, LANES if coarse else 2 * LANES), BF16),
                pltpu.VMEM((rows_here, LANES), F32),
            ],
            col_at,
            bnd_rows,
            block_rows,
            packed,
            group.reshape(n_row, LB, HALF, LANES),
            bnd_all,
            landed,
            *((shard_p, group_p.reshape(n_row, LB, HALF, LANES), bnd_p, landed_p) if sweep == 0 else ()),
            current,
            image_x,
            basis,
        )
        gram = sum_all(3 + 2 * sweep, n_sub, n_row, gram)
        if sweep < ITERS - 1:
            metric, current, image_x, basis, packed, bnd, parts = plain(
                functools.partial(step_kernel, total_rows),
                "step",
                [SMEM] * 3 + [VMEM] * 8,
                [shape(KB, LANES), shape(rows_here, LANES), shape(rows_here, LANES), shape(rows_here, LANES), *sent(1, BF16)],
                solver,
                *faces,
                gram,
                metric,
                if_val,
                weights,
                current,
                image_x,
                basis,
                image_b,
            )
    modes, search = plain(
        functools.partial(last_kernel, total_rows),
        "last",
        [VMEM] * 4,
        [shape(KB, rows_here), shape(KB, rows_here)],
        solver,
        gram,
        metric,
        current,
        basis,
    )
    return modes.T, search.T


def solution(mesh):
    n_sub, n_row = mesh.shape["sub"], mesh.shape["row"]
    ny = 4 if n_row == 16 else 2
    return jax.shard_map(
        functools.partial(local, (n_sub, ny, n_row // ny)),
        mesh=mesh,
        in_specs=(
            P(("sub", "row"), None),
            P(("sub", "row"), None),
            P(("sub", "row")),
            P("sub", "row", None),
            P("sub", "row", None),
            P("sub", "row", None, None, None),
            P("sub", "row", None),
            P("sub", "row", None),
            P("sub", "row", None),
            P("sub", "row", None, None, None),
        ),
        out_specs=(P(("sub", "row"), None), P(("sub", "row"), None)),
        check_vma=False,
    )
```

```python
import functools

import jax
import jax.numpy as jnp
from jax import lax
from jax.experimental import pallas as pl
from jax.experimental.pallas import tpu as pltpu
from jax.sharding import PartitionSpec as P

KB = 64
LB = 12
IFR = 3
ITERS = 2
GROUPS = 8
HALF = KB // 2
SLOTS = 2 * GROUPS
LANES = 128
MESH = pl.DeviceIdType.MESH
F32, BF16 = jnp.float32, jnp.bfloat16
VMEM = pl.BlockSpec(memory_space=pltpu.VMEM)
SMEM = pl.BlockSpec(memory_space=pltpu.SMEM)
ANY = pl.BlockSpec(memory_space=pl.ANY)
LIMIT = 12 * 1024 * 1024
SMALL = 4 * 1024 * 1024
EARLY = 4 * LB


def hdot(a, b):
    return jnp.dot(a, b, precision=lax.Precision.HIGHEST, preferred_element_type=F32)


def swap(v):
    return pltpu.roll(v, LANES // 2, 1)


def is_left(shape):
    return lax.broadcasted_iota(jnp.int32, shape, 1) < LANES // 2


def pack(block):
    left = is_left((HALF, LANES))
    return jnp.where(left, block[:HALF], swap(block[HALF:]))


def two_terms(v):
    hi = v.astype(BF16)
    return hi, (v - hi.astype(F32)).astype(BF16)


def add_terms(coarse, product, v):
    if coarse:
        return product
    at = 2 * v * LANES
    return product[:, at : at + LANES] + product[:, at + LANES : at + 2 * LANES]


def write_messages(many, coarse, shard, bnd_out, parts, bnd, face_row, face_src, face_val):
    for q in range(IFR):
        bnd_out[q] = shard[bnd[0, 0, q]]
    parts[...] = jnp.zeros_like(parts)
    left = is_left((HALF, LANES))
    products = []
    for k in range(LB):
        block = shard[face_row[0, 0, k]]
        face = face_val[0, 0, k]
        if coarse:
            terms = block
        else:
            terms = jnp.concatenate([t for v in range(many) for t in two_terms(block[v * HALF : (v + 1) * HALF])], 1)
        one, two = (
            lax.dot_general(half, terms, (((0,), (0,)), ((), ())), preferred_element_type=F32)
            for half in (face[:HALF], face[HALF:])
        )
        sums = []
        for v in range(many):
            first, second = add_terms(coarse, one, v), add_terms(coarse, two, v)
            sums.append(
                jnp.where(left, first[:HALF] + swap(second[:HALF]), swap(first[HALF:]) + second[HALF:])
            )
        products.append(jnp.concatenate(sums, 0) if many > 1 else sums[0])
    for k in range(LB):
        source = face_src[0, 0, k]
        target, slot = source // IFR, source % IFR
        core, z = target % 2, target // 2
        parts[core, z, slot] = parts[core, z, slot] + products[k]


def start_kernel(bnd, face_row, face_src, modes, search, precond, face_val, current, *refs):
    first, second, weights = refs[:3], refs[3:6], refs[6]
    current[...] = jnp.concatenate([modes[...], search[...]], 0).T
    for a in range(LB):
        block = current[a * KB : (a + 1) * KB]
        first[0][a] = pack(block)
        second[0][a] = pack(swap(block))
    for c in range(LB * KB // LANES):
        weights[c * LANES : (c + 1) * LANES] = jnp.broadcast_to(precond[c : c + 1], (LANES, LANES)).T
    write_messages(1, False, *first, bnd, face_row, face_src, face_val)
    write_messages(1, False, *second, bnd, face_row, face_src, face_val)


def exchange_steps(greet, count, handing, ny, nx, n_sub, *refs):
    arrays = count + 2 * handing
    shards, bnd, parts = refs[:arrays], refs[arrays], refs[arrays + 1]
    groups, bnd_all, landed = refs[arrays + 2 : 2 * arrays + 2], refs[2 * arrays + 2], refs[2 * arrays + 3]
    theirs, ours, sub_send, sub_recv, row_send, row_recv, ring_send, ring_recv = refs[2 * arrays + 4 :]
    sub, row = lax.axis_index("sub"), lax.axis_index("row")
    y, x = row // nx, row % nx
    nz = n_sub // 2
    z, core = sub // 2, sub % 2
    sibling = z * 2 + 1 - core

    def at(dy, dx):
        return ((y + dy + ny) % ny) * nx + (x + dx + nx) % nx

    def along(d):
        return ((z + d + nz) % nz) * 2 + core

    if greet:
        barrier = pltpu.get_barrier_semaphore()
        for d in range(1, nx):
            pl.semaphore_signal(barrier, inc=1, device_id={"row": at(0, d)}, device_id_type=MESH)
        for d in range(1, ny):
            pl.semaphore_signal(barrier, inc=1, device_id={"row": at(d, 0)}, device_id_type=MESH)
        for d in range(1, nz):
            pl.semaphore_signal(barrier, inc=1, device_id={"sub": along(d)}, device_id_type=MESH)
        pl.semaphore_signal(barrier, inc=1, device_id={"sub": sibling}, device_id_type=MESH)
        pl.semaphore_wait(barrier, nx - 1 + ny - 1 + nz)

    def to_sub(src, dst, kind, d, target):
        return pltpu.make_async_remote_copy(
            src_ref=src,
            dst_ref=dst,
            send_sem=sub_send.at[kind, d],
            recv_sem=sub_recv.at[kind, d],
            device_id={"sub": target},
            device_id_type=MESH,
        )

    def landed_at(ref, sem):
        pltpu.make_async_copy(ref, ref, sem).wait()

    def hop(i, half, holder, src, to, sem):
        size = shards[i].shape[0] // 2
        return pltpu.make_async_remote_copy(
            src_ref=src,
            dst_ref=groups[i].at[holder, pl.ds(half * size, size)],
            send_sem=row_send.at[i, half, sem],
            recv_sem=row_recv.at[i, half, sem],
            device_id={"row": to},
            device_id_type=MESH,
        )

    def half_of(i, half, holder=None):
        size = shards[i].shape[0] // 2
        part = pl.ds(half * size, size)
        return shards[i].at[part] if holder is None else groups[i].at[holder, part]

    counts = ((nx, ny), (ny, nx))

    def place(half, first, second):
        return at(second, first) if half == 0 else at(first, second)

    sends = []

    def send(copy):
        copy.start()
        sends.append(copy)

    send(to_sub(parts.at[1 - core], theirs, 3, 0, sibling))
    for i in range(count):
        for half in range(2):
            n1, n2 = counts[half]
            for first in range(1, n1):
                send(hop(i, half, row, half_of(i, half), place(half, first, 0), first * n2))
        if i == 0:
            for d in range(1, nz):
                send(to_sub(bnd, bnd_all.at[sub], 0, d, along(d)))
            send(to_sub(bnd, bnd_all.at[sub], 1, 0, sibling))
        for half in range(2):
            n1, n2 = counts[half]
            for second in range(1, n2):
                send(hop(i, half, row, half_of(i, half), place(half, 0, second), second))

    for axis in range(2 * handing):
        mine, n = (y, x)[axis], (ny, nx)[axis]
        for d in range(1, n):
            t = (mine + d) % n
            send(
                pltpu.make_async_remote_copy(
                    src_ref=shards[count + axis].at[t],
                    dst_ref=groups[count + axis].at[mine],
                    send_sem=ring_send.at[axis, d],
                    recv_sem=ring_recv.at[axis, d],
                    device_id={"row": (t * nx + x, y * nx + t)[axis]},
                    device_id_type=MESH,
                )
            )

    yield
    landed_at(theirs, sub_recv.at[3, 0])
    ours[...] = theirs[...] + parts[core]
    for d in range(1, nz):
        send(to_sub(ours.at[(z + d) % nz], landed.at[z], 2, d, along(d)))
    landed[z] = ours[z]

    for i in range(count):
        for first in range(1, max(nx, ny)):
            for half in range(2):
                n1, n2 = counts[half]
                if first >= n1:
                    continue
                holder = place(half, -first, 0)
                landed_at(half_of(i, half, holder), row_recv.at[i, half, first * n2])
                for second in range(1, n2):
                    send(hop(i, half, holder, half_of(i, half, holder), place(half, 0, second), first * n2 + second))
        if i == 0:
            for d in range(1, nz):
                here = bnd_all.at[along(-d)]
                landed_at(here, sub_recv.at[0, d])
                send(to_sub(here, here, 1, d, sibling))
    yield
    for d in range(1, nz):
        landed_at(landed.at[(z + nz - d) % nz], sub_recv.at[2, d])
    for d in range(nz):
        landed_at(bnd_all.at[((z + nz - d) % nz) * 2 + 1 - core], sub_recv.at[1, d])
    for i in range(count):
        for half in range(2):
            n1, n2 = counts[half]
            for first in range(n1):
                for second in range(1, n2):
                    landed_at(half_of(i, half, place(half, -first, -second)), row_recv.at[i, half, first * n2 + second])
    for axis in range(2 * handing):
        mine, n = (y, x)[axis], (ny, nx)[axis]
        for d in range(1, n):
            landed_at(groups[count + axis].at[(mine + n - d) % n], ring_recv.at[axis, d])
    for copy in sends:
        copy.wait_send()


def exchange_kernel(*args):
    for _ in exchange_steps(True, *args):
        pass


def exchange_scratch(count, ny, nx, parts):
    most, n_row = max(parts.shape[1], 2), ny * nx
    return [
        pltpu.VMEM(parts.shape[1:], F32),
        pltpu.VMEM(parts.shape[1:], F32),
        pltpu.SemaphoreType.DMA((4, most)),
        pltpu.SemaphoreType.DMA((4, most)),
        pltpu.SemaphoreType.DMA((count, 2, n_row)),
        pltpu.SemaphoreType.DMA((count, 2, n_row)),
        pltpu.SemaphoreType.DMA((2, max(nx, ny))),
        pltpu.SemaphoreType.DMA((2, max(nx, ny))),
    ]


def exchange(collective_id, ny, nx, shards, handed, bnd, parts):
    count, n_row = len(shards), ny * nx
    nz = parts.shape[1]
    n_sub = 2 * nz
    gathered = [jax.ShapeDtypeStruct((n_row, *a.shape), a.dtype) for a in shards]
    gathered += [jax.ShapeDtypeStruct((n, *a.shape[1:]), a.dtype) for n, a in zip((ny, nx), handed)]
    return pl.pallas_call(
        functools.partial(exchange_kernel, count, bool(handed), ny, nx, n_sub),
        name=f"exchange_{collective_id}",
        out_shape=gathered
        + [jax.ShapeDtypeStruct((n_sub, *bnd.shape), bnd.dtype), jax.ShapeDtypeStruct(parts.shape[1:], F32)],
        in_specs=[VMEM] * (len(gathered) + 2),
        out_specs=[VMEM] * (len(gathered) + 2),
        scratch_shapes=exchange_scratch(count, ny, nx, parts),
        compiler_params=pltpu.CompilerParams(
            collective_id=collective_id, has_side_effects=True, vmem_limit_bytes=SMALL
        ),
    )(*shards, *handed, bnd, parts)


def rings_kernel(ny, nx, codes, early, late, codes_all, ring_x, ring_y, send, recv):
    row = lax.axis_index("row")
    y, x = row // nx, row % nx
    n_row = ny * nx
    barrier = pltpu.get_barrier_semaphore()
    for d in range(1, n_row):
        pl.semaphore_signal(barrier, inc=1, device_id={"row": (row + d) % n_row}, device_id_type=MESH)
    pl.semaphore_wait(barrier, n_row - 1)
    rings = (
        (nx, x, lambda t: y * nx + t, early, ring_x),
        (ny, y, lambda t: t * nx + x, late, ring_y),
        (n_row, row, lambda t: t, codes, codes_all),
    )
    sends = []
    order = [(2, d) for d in range(1, n_row)]
    for d in range(1, max(nx, ny)):
        order += [(i, (d, rings[i][0] - d)[i]) for i in range(2) if d < rings[i][0]]
    for i, d in order:
        n, mine, name, src, dst = rings[i]
        copy = pltpu.make_async_remote_copy(
            src_ref=src,
            dst_ref=dst.at[mine],
            send_sem=send.at[i, d],
            recv_sem=recv.at[i, d],
            device_id={"row": name((mine + d) % n)},
            device_id_type=MESH,
        )
        copy.start()
        sends.append(copy)
    codes_all[row] = codes[...]
    for i, (n, mine, _, _, dst) in enumerate(rings):
        for d in range(1, n):
            here = dst.at[(mine + n - d) % n]
            pltpu.make_async_copy(here, here, recv.at[i, d]).wait()
    for copy in sends:
        copy.wait_send()


def ring_gather(collective_id, ny, nx, codes, early, late):
    return pl.pallas_call(
        functools.partial(rings_kernel, ny, nx),
        name=f"rings_{collective_id}",
        out_shape=[
            jax.ShapeDtypeStruct((n, *a.shape), a.dtype) for n, a in ((ny * nx, codes), (nx, early), (ny, late))
        ],
        in_specs=[VMEM] * 3,
        out_specs=[VMEM] * 3,
        scratch_shapes=[pltpu.SemaphoreType.DMA((3, ny * nx))] * 2,
        compiler_params=pltpu.CompilerParams(
            collective_id=collective_id, has_side_effects=True, vmem_limit_bytes=SMALL
        ),
    )(codes, early, late)


def sum_steps(n_sub, n_row, make, parts, out, by_row, by_sub, own_sem, send, recv):
    sub, row = lax.axis_index("sub"), lax.axis_index("row")
    barrier = pltpu.get_barrier_semaphore()

    @pl.loop(1, n_row)
    def _(d):
        pl.semaphore_signal(barrier, inc=1, device_id={"row": (row + d) % n_row}, device_id_type=MESH)

    @pl.loop(1, n_sub)
    def _(d):
        pl.semaphore_signal(barrier, inc=1, device_id={"sub": (sub + d) % n_sub}, device_id_type=MESH)

    make()
    pl.semaphore_wait(barrier, n_row - 1 + n_sub - 1)

    def phase(index, axis, mine, n, source, target):
        def to(d):
            t = (mine + d) % n
            return pltpu.make_async_remote_copy(
                src_ref=source(t),
                dst_ref=target(mine),
                send_sem=send.at[index, d],
                recv_sem=recv.at[index, d],
                device_id={axis: t},
                device_id_type=MESH,
            )

        own = pltpu.make_async_copy(source(mine), target(mine), own_sem.at[index])

        @pl.loop(1, n)
        def _(d):
            to(d).start()

        own.start()
        yield

        @pl.loop(1, n)
        def _(d):
            here = target((mine + n - d) % n)
            pltpu.make_async_copy(here, here, recv.at[index, d]).wait()
            to(d).wait_send()

        own.wait()

    def summed(buffer, n):
        total = buffer[0]
        for t in range(1, n):
            total = total + buffer[t]
        return total

    yield from phase(0, "row", row, n_row, lambda t: parts.at[t], lambda t: by_row.at[t])
    by_row[n_row] = summed(by_row, n_row)
    yield from phase(1, "sub", sub, n_sub, lambda t: by_row.at[n_row], lambda t: by_sub.at[t])
    by_sub[n_sub] = summed(by_sub, n_sub)
    yield from phase(2, "row", row, n_row, lambda t: by_sub.at[n_sub], lambda t: out.at[t])


def gram_of(current, image_x, basis, image_b, diagonal=None):
    y = basis[...]
    turned = y.T
    left = is_left(y.shape)
    if diagonal is None:
        energy = hdot(turned, image_b[...])
    else:
        twice = jnp.where(left, y + (y - y.astype(BF16).astype(F32)), 0.0)
        energy = hdot(turned, jnp.where(left, diagonal[...], image_x[...])) + hdot(
            twice.T, jnp.where(left, image_b[...], 0.0)
        )
    driving = hdot(turned, jnp.where(left, image_x[...], swap(current[...])))
    return jnp.concatenate([energy, driving, hdot(turned, y)], 0)


def sum_kernel(count, n_sub, n_row, *refs):
    images, out, parts, scratch = refs[:count], refs[count], refs[count + 1], refs[count + 2 :]
    rows = parts.shape[1]

    def make():
        gram = gram_of(*images)
        for t in range(n_row):
            parts[t] = gram[t * rows : (t + 1) * rows]

    for _ in sum_steps(n_sub, n_row, make, parts, out, *scratch):
        pass


def sum_scratch(n_sub, n_row, rows):
    most = max(n_sub, n_row)
    return [
        pltpu.VMEM((n_row + 1, rows, LANES), F32),
        pltpu.VMEM((n_sub + 1, rows, LANES), F32),
        pltpu.SemaphoreType.DMA((3,)),
        pltpu.SemaphoreType.DMA((3, most)),
        pltpu.SemaphoreType.DMA((3, most)),
    ]


def sum_grams(collective_id, n_sub, n_row, images):
    rows = 3 * LANES // n_row
    total = pl.pallas_call(
        functools.partial(sum_kernel, len(images), n_sub, n_row),
        name=f"sum_{collective_id}",
        out_shape=shape(n_row, rows, LANES),
        in_specs=[VMEM] * len(images),
        out_specs=VMEM,
        scratch_shapes=[pltpu.VMEM((n_row, rows, LANES), F32)] + sum_scratch(n_sub, n_row, rows),
        compiler_params=pltpu.CompilerParams(
            collective_id=collective_id, has_side_effects=True, vmem_limit_bytes=LIMIT
        ),
    )(*images)
    return total.reshape(-1, LANES)


def sum_beside_exchange_kernel(ny, nx, n_sub, part, shard, bnd, parts, total, group, bnd_all, landed, *scratch):
    summing = sum_steps(n_sub, ny * nx, lambda: None, part, total, *scratch[:5])
    moving = exchange_steps(
        False, 1, False, ny, nx, n_sub, shard, bnd, parts, group, bnd_all, landed, *scratch[5:]
    )
    for _ in range(3):
        next(summing)
        next(moving, None)
    for _ in summing:
        pass


def sum_beside_exchange(collective_id, ny, nx, part, shard, bnd, parts):
    n_row = ny * nx
    n_sub = 2 * parts.shape[1]
    rows = part.shape[0] // n_row
    total, *moved = pl.pallas_call(
        functools.partial(sum_beside_exchange_kernel, ny, nx, n_sub),
        name=f"sum_beside_exchange_{collective_id}",
        out_shape=[
            shape(n_row, rows, LANES),
            shape(n_row, *shard.shape),
            shape(n_sub, *bnd.shape),
            shape(*parts.shape[1:]),
        ],
        in_specs=[VMEM] * 4,
        out_specs=[VMEM] * 4,
        scratch_shapes=sum_scratch(n_sub, n_row, rows) + exchange_scratch(1, ny, nx, parts),
        compiler_params=pltpu.CompilerParams(
            collective_id=collective_id, has_side_effects=True, vmem_limit_bytes=SMALL
        ),
    )(part.reshape(n_row, rows, LANES), shard, bnd, parts)
    return total.reshape(part.shape), *moved


def select_kernel(ny, nx, codes, own_val, ring_x, ring_y, to_y, to_x, back_at, flat, goes, goes_at, sem):
    row = lax.axis_index("row")
    y, x = row // nx, row % nx
    late = LB * GROUPS - LB - EARLY
    flat[...] = codes[:, 0, :]
    value = flat[...]
    owner, within = value // 256, value // 16 % 16
    at = lax.broadcasted_iota(jnp.int32, value.shape, 1)
    member = jnp.zeros_like(at)
    for g in range(1, GROUPS):
        member = member + jnp.where(at >= g * LB, LB, 0)
    by_x = jnp.where(owner % nx == x, owner // nx, ny) * EARLY + member - LB + within
    by_y = jnp.where(owner // nx == y, owner % nx, nx) * late + member - LB - EARLY + within
    goes[...] = jnp.where(at < LB + EARLY, by_x, by_y)
    copy = pltpu.make_async_copy(goes, goes_at, sem)
    copy.start()
    copy.wait()

    def scatter(device, source, start, size, out):
        @pl.loop(0, size // LB)
        def _(g):
            for b in range(LB):
                k = g * LB + b
                out[goes_at[device, start + k]] = source(k)

    scatter(row, lambda k: own_val[LB + k], LB, EARLY, to_y)
    scatter(row, lambda k: own_val[LB + EARLY + k], LB + EARLY, late, to_x)

    @pl.loop(1, nx)
    def _(d):
        t = (x + d) % nx
        scatter(y * nx + t, lambda k: ring_x[t, k], LB, EARLY, to_y)

    @pl.loop(1, ny)
    def _(d):
        t = (y + d) % ny
        scatter(t * nx + x, lambda k: ring_y[t, k], LB + EARLY, late, to_x)

    code = flat[...]
    lane = lax.broadcasted_iota(jnp.int32, code.shape, 1)
    device = lax.broadcasted_iota(jnp.int32, code.shape, 0)
    ours = (code // 256 == row) & (lane >= LB) & (lane < GROUPS * LB)
    value = device * 16 + code % 16
    place = code // 16 % 16
    lines = [jnp.sum(jnp.where(ours & (place == a), value, 0), axis=0, keepdims=True) for a in range(LB)]
    lines += [jnp.zeros_like(lines[0])] * (16 - LB)
    k = lax.broadcasted_iota(jnp.int32, (LANES, LANES), 0)
    g = lax.broadcasted_iota(jnp.int32, (LANES, LANES), 1)
    member = ((k >= g * LB) & (k < g * LB + LB)).astype(F32)
    back_at[...] = hdot(jnp.concatenate(lines, 0).astype(F32), member).astype(jnp.int32)


def build_kernel(
    ny, nx, in_row, in_col, back_at, face_row, face_src, own_val, to_y, to_x, from_y, from_x, face_val, rows_ref, col_at,
    own_at, face_at
):
    n_row = ny * nx
    row = lax.axis_index("row")
    y, x = row // nx, row % nx

    @pl.loop(0, GROUPS)
    def _(g):
        for b in range(LB):
            k = g * LB + b
            own_at[g * LB + in_row[0, 0, k]] = k

    for k in range(LB):
        face_at[face_row[0, 0, k]] = k

    quarter = lax.broadcasted_iota(jnp.int32, (KB, LANES), 1) % KB < HALF
    left = is_left((HALF, LANES))

    def pair(one, two):
        top = jnp.where(left, one, swap(two))
        low = jnp.where(left, swap(one), two)
        return jnp.concatenate([top, low], 0)

    @pl.loop(0, LB)
    def _(a):
        def put(slot, ij, kl):
            lanes = slice(slot * LANES, (slot + 1) * LANES)
            rows_ref[a, :KB, lanes] = jnp.where(quarter, ij, pltpu.roll(kl, HALF, 1)).astype(BF16)
            rows_ref[a, KB:, lanes] = jnp.where(quarter, pltpu.roll(ij, LANES - HALF, 1), kl).astype(BF16)

        own = []
        for g in range(GROUPS):
            k = own_at[g * LB + a]
            col_at[a * SLOTS + g] = in_col[0, 0, k]
            own.append(own_val[k].astype(F32))
        put(0, pair(own[0], own[2]), pair(own[1], own[3]))
        put(1, pair(own[4], own[6]), pair(own[5], own[7]))
        back = []
        for g in range(GROUPS - 1):
            code = back_at[a, g + 1]
            device = code // 16
            col_at[a * SLOTS + GROUPS + g] = device * LB + code % 16
            if (g + 1) * LB <= EARLY:
                slot, t, mine, kept, got = g * LB + a, device // nx, y, to_y, from_y
            else:
                slot, t, mine, kept, got = g * LB - EARLY + a, device % nx, x, to_x, from_x
            back.append(jnp.where(t == mine, kept[mine, slot].astype(F32), got[t, slot].astype(F32)))
        turned = jnp.concatenate([pair(back[0], back[1]), pair(back[2], back[3])], 0).T
        put(2, turned[:KB], turned[KB:])
        turned = jnp.concatenate([pair(back[4], back[5]), pair(back[6], back[6])], 0).T
        k = face_at[a]
        col_at[a * SLOTS + SLOTS - 1] = n_row * LB + face_src[0, 0, k]
        face = face_val[0, 0, k].astype(F32)
        put(3, turned[:KB], jnp.where(is_left((KB, LANES)), turned[KB:], jnp.concatenate([face, face], 1)))


def apply_operator(many, coarse, col_at, rows_ref, own, group, bnd_all, terms, put_row):
    n_row, n_sub = group.shape[0], bnd_all.shape[0]

    def split(values, at, size):
        if coarse:
            terms[pl.ds(at, size)] = values
            return
        for v in range(many):
            hi, mid = two_terms(values[:, v * HALF : (v + 1) * HALF])
            lane = 2 * v * LANES
            terms[pl.ds(at, size), :, lane : lane + LANES] = hi
            terms[pl.ds(at, size), :, lane + LANES : lane + 2 * LANES] = mid

    @pl.loop(0, n_row)
    def _(r):
        split(group[r], r * LB, LB)

    split(own[...], lax.axis_index("row") * LB, LB)

    @pl.loop(0, n_sub)
    def _(t):
        split(bnd_all[t], n_row * LB + t * IFR, IFR)

    together = 3

    @pl.loop(0, LB // together)
    def _(c):
        for i in range(together):
            a = c * together + i
            total = None
            for part in range(2):
                here = range(part * GROUPS, (part + 1) * GROUPS)
                pieces = [terms[col_at[a * SLOTS + t]] for t in here]
                if coarse and part == 0:
                    pieces[0] = jnp.zeros_like(pieces[0])
                stack = jnp.concatenate(pieces, 0)
                lhs = rows_ref[a, :, part * GROUPS * HALF : (part + 1) * GROUPS * HALF]
                product = jnp.dot(lhs, stack, preferred_element_type=F32)
                total = product if total is None else total + product
            blocks = []
            for v in range(many):
                both = add_terms(coarse, total, v)
                blocks.append(both[:KB] + swap(both[KB:]))
            put_row(a, blocks)


def landed_blocks(many, landed, q):
    total = landed[0, q]
    for t in range(1, landed.shape[0]):
        total = total + landed[t, q]
    parts = [total[v * HALF : (v + 1) * HALF] for v in range(many)]
    return [jnp.concatenate([part, swap(part)], 0) for part in parts]


def block_at(a):
    return pl.ds(pl.multiple_of(a * KB, KB), KB)


def first_apply_kernel(col_at, bnd, rows_ref, own, group, bnd_all, landed, basis, image, gram, terms):
    left_block = is_left((KB, LANES))

    def put_row(a, blocks):
        image[block_at(a), :] = jnp.where(left_block, blocks[0], 0.0)

    apply_operator(1, False, col_at, rows_ref, own, group, bnd_all, terms, put_row)
    for q in range(IFR):
        at = block_at(bnd[0, 0, q])
        image[at, :] = image[at, :] + jnp.where(left_block, landed_blocks(1, landed, q)[0], 0.0)
    both = basis[...]
    left = is_left(both.shape)
    gram[...] = hdot(both.T, jnp.where(left, both, swap(image[...])))


def apply_kernel(coarse, col_at, bnd, rows_ref, own, group, bnd_all, landed, *refs):
    *search, image_x, basis, image_b, diagonal, terms = refs if coarse else (*refs[:-1], None, refs[-1])
    left_block = is_left((KB, LANES))
    source = image_x
    if search:
        source = image_b

        def put_search(a, blocks):
            image_b[block_at(a), :] = swap(blocks[0])

        apply_operator(1, False, col_at, rows_ref, *search[:3], terms, put_search)
        for q in range(IFR):
            at = block_at(bnd[0, 0, q])
            image_b[at, :] = image_b[at, :] + jnp.where(left_block, 0.0, swap(landed_blocks(1, search[3], q)[0]))

    def put_row(a, blocks):
        at = block_at(a)
        image_b[at, :] = jnp.where(left_block, blocks[0], source[at, :])

    apply_operator(1, coarse, col_at, rows_ref, own, group, bnd_all, terms, put_row)
    for q in range(IFR):
        at = block_at(bnd[0, 0, q])
        image_b[at, :] = image_b[at, :] + jnp.where(left_block, landed_blocks(1, landed, q)[0], 0.0)
    if coarse:
        for a in range(LB):
            own_terms = jnp.concatenate(two_terms(pack(basis[a * KB : (a + 1) * KB, :])), 1)
            product = jnp.dot(rows_ref[a, :, :HALF], own_terms, preferred_element_type=F32)
            both = add_terms(False, product, 0)
            diagonal[a * KB : (a + 1) * KB] = both[:KB] + swap(both[KB:])


def eliminate(work, n, full):
    lane = lax.broadcasted_iota(jnp.int32, (n, LANES), 1)
    line = lax.broadcasted_iota(jnp.int32, (n, 1), 0)
    lane1 = lax.broadcasted_iota(jnp.int32, (1, LANES), 1)

    def step(t, pivots):
        j = 2 * t
        k = j + 1
        row0, row1 = work[pl.ds(j, 1), :], work[pl.ds(k, 1), :]
        whole = work[...]

        def entry(row, at):
            return jnp.sum(jnp.where(lane1 == at, row[:, :LANES], 0.0), axis=1, keepdims=True)

        def column(at):
            return jnp.sum(jnp.where(lane == at, whole[:, :LANES], 0.0), axis=1, keepdims=True)

        a, b, c, d = entry(row0, j), entry(row0, k), entry(row1, j), entry(row1, k)
        col0, col1 = column(j), column(k)
        inverse = 1.0 / a
        ratio = b * inverse
        below = row1 - (c * inverse) * row0
        second = d - c * ratio
        unit1 = below * (1.0 / second)
        unit0 = row0 * inverse - ratio * unit1
        moved = whole - (col0 * unit0 + col1 * unit1)
        if full:
            work[...] = jnp.where(line == j, unit0, jnp.where(line == k, unit1, moved))
        else:
            work[...] = jnp.where(line > k, moved, jnp.where(line == k, below, whole))
        return jnp.where(line == j, a, jnp.where(line == k, second, pivots))

    return lax.fori_loop(0, n // 2, step, jnp.zeros((n, 1), F32))


def padded(top):
    return jnp.concatenate([top, jnp.zeros_like(top)], 0)


def identity_right():
    line = lax.broadcasted_iota(jnp.int32, (KB, LANES), 0)
    lane = lax.broadcasted_iota(jnp.int32, (KB, LANES), 1)
    return (lane == line + KB).astype(F32)


def identity_left():
    line = lax.broadcasted_iota(jnp.int32, (KB, LANES), 0)
    lane = lax.broadcasted_iota(jnp.int32, (KB, LANES), 1)
    return (lane == line).astype(F32)


CHUNK = 256


def chunks(body):
    @pl.loop(0, LB * KB // CHUNK)
    def _(c):
        body(pl.ds(pl.multiple_of(c * CHUNK, CHUNK), CHUNK))


def new_basis(ritz, precond, current, image_x, basis, update, at):
    here = current[at, :]
    left = is_left(here.shape)
    residue = jnp.where(left, image_x[at, :], 0.0) - hdot(here, ritz)
    fresh = precond[at, :] * residue
    update[at, :] = fresh
    basis[at, :] = jnp.where(left, fresh, here)


def send_basis(coarse, update, packed, bnd_out, parts, bnd, face_row, face_src, face_val):
    for a in range(LB):
        packed[a] = pack(update[a * KB : (a + 1) * KB, :]).astype(packed.dtype)
    write_messages(1, coarse, packed, bnd_out, parts, bnd, face_row, face_src, face_val)


def first_ritz_kernel(
    bnd, face_row, face_src, gram, face_val, precond, current, image_x, basis, packed, bnd_out, parts, update, work
):
    work[...] = gram[:KB]
    eliminate(work, KB, True)
    left = is_left((KB, LANES))
    ritz = padded(jnp.where(left, swap(work[...]), 0.0))
    chunks(lambda at: new_basis(ritz, precond, current, image_x, basis, update, at))
    send_basis(False, update, packed, bnd_out, parts, bnd, face_row, face_src, face_val)


def combine(total_rows, gram, metric, wide, narrow):
    energy = gram[0:LANES]
    turned = energy.T
    upper = lax.broadcasted_iota(jnp.int32, (LANES, LANES), 0) < KB
    right_half = lax.broadcasted_iota(jnp.int32, (LANES, LANES), 1) >= KB
    crossed = jnp.where(upper, energy, turned)
    wide[:, :LANES] = jnp.where(upper == right_half, crossed, 0.5 * (energy + turned))
    right = gram[LANES : 2 * LANES]
    wide[:, LANES:] = right
    eliminate(wide, LANES, True)
    left_all = is_left((LANES, LANES))
    left = is_left((KB, LANES))
    z = jnp.where(left_all, -wide[:, LANES:], 0.0)
    cross = hdot(right.T, z)
    against = jnp.where(left_all, swap(right), 0.0) + hdot(gram[2 * LANES :], z)
    square = hdot(z.T, against)[:KB]
    lengths = jnp.where(left, metric[...], 0.0) + cross[KB:] + square
    narrow[...] = lengths * (1.0 / total_rows) + identity_right()
    pivots = eliminate(narrow, KB, False)
    root = 1.0 / jnp.sqrt(pivots)
    inverse = padded(jnp.where(left, swap(narrow[...]), 0.0) * root)
    turned = inverse.T
    half = hdot(z, turned)
    energy = jnp.where(left, swap(metric[...]), 0.0) + cross[:KB]
    energy = hdot(hdot(inverse, padded(energy)), turned)
    return turned, jnp.where(left_all, half, swap(half)), energy


def step_kernel(
    total_rows,
    bnd,
    face_row,
    face_src,
    gram,
    metric,
    face_val,
    precond,
    current,
    image_x,
    basis,
    image_b,
    next_metric,
    next_current,
    next_image,
    next_basis,
    packed,
    bnd_out,
    parts,
    update,
    wide,
    narrow,
):
    turned, moves, energy = combine(total_rows, gram, metric, wide, narrow)
    next_metric[...] = identity_left() * total_rows + swap(energy[:KB])
    ritz = energy * (1.0 / total_rows)

    def body(at):
        next_current[at, :] = hdot(current[at, :], turned) + hdot(basis[at, :], moves)
        next_image[at, :] = hdot(image_x[at, :], turned) + hdot(image_b[at, :], moves)
        new_basis(ritz, precond, next_current, next_image, next_basis, update, at)

    chunks(body)
    send_basis(True, update, packed, bnd_out, parts, bnd, face_row, face_src, face_val)


def last_kernel(total_rows, gram, metric, current, basis, modes, search, both, wide, narrow):
    turned, moves, _ = combine(total_rows, gram, metric, wide, narrow)

    def body(at):
        both[at, :] = hdot(current[at, :], turned) + hdot(basis[at, :], moves)

    chunks(body)
    whole = both[...].T
    modes[...] = whole[:KB]
    search[...] = whole[KB:]


def plain(kernel, name, specs, outs, scratch, *args):
    return pl.pallas_call(
        kernel,
        name=name,
        out_shape=outs,
        in_specs=specs,
        out_specs=[VMEM] * len(outs),
        scratch_shapes=scratch,
        compiler_params=pltpu.CompilerParams(vmem_limit_bytes=LIMIT),
    )(*args)


def shape(*dims):
    return jax.ShapeDtypeStruct(dims, F32)


def local(grid, modes, search, precond, in_row, in_col, in_val, bnd_rows, if_row, if_src, if_val):
    n_sub, ny, nx = grid
    n_row = ny * nx
    rows_here = LB * KB
    total_rows = float(rows_here * n_sub * n_row)
    vals = in_val[0, 0]
    own_val = jnp.concatenate([vals[:, :HALF], vals[:, HALF:]], 2)
    faces = (bnd_rows, if_row, if_src)

    def sent(many, kind=F32):
        return [
            jax.ShapeDtypeStruct((LB, many * HALF, LANES), kind),
            jax.ShapeDtypeStruct((IFR, many * HALF, LANES), kind),
            shape(2, n_sub // 2, IFR, many * HALF, LANES),
        ]

    current, shard, bnd, parts, shard_p, bnd_p, parts_p, weights = plain(
        start_kernel,
        "start",
        [SMEM] * 3 + [VMEM] * 4,
        [shape(rows_here, LANES), *sent(1), *sent(1), shape(rows_here, LANES)],
        [],
        *faces,
        modes.T,
        search.T,
        precond.reshape(-1, LANES),
        if_val,
    )
    cols = in_col[0]
    codes = cols // LB * 256 + cols % LB * 16 + in_row[0]
    codes = jnp.pad(codes, ((0, 7), (0, LANES - GROUPS * LB)))
    early = own_val[LB : LB + EARLY].reshape(-1, LANES)
    late = own_val[LB + EARLY :].reshape(-1, LANES)
    codes_all, ring_x, ring_y = ring_gather(6, ny, nx, codes, early, late)
    in_early, in_late = EARLY, GROUPS * LB - LB - EARLY

    def blocks(count):
        return jax.ShapeDtypeStruct((count, HALF, LANES), BF16)

    to_y, to_x, back_at = plain(
        functools.partial(select_kernel, ny, nx),
        "select",
        [VMEM] * 4,
        [blocks((ny + 1) * in_early), blocks((nx + 1) * in_late), jax.ShapeDtypeStruct((16, LANES), jnp.int32)],
        [pltpu.VMEM((n_row, LANES), jnp.int32)] * 2
        + [pltpu.SMEM((n_row, LANES), jnp.int32), pltpu.SemaphoreType.DMA],
        codes_all,
        own_val,
        ring_x.reshape(nx, in_early, HALF, LANES),
        ring_y.reshape(ny, in_late, HALF, LANES),
    )
    to_y = to_y.reshape(ny + 1, in_early, HALF, LANES)
    to_x = to_x.reshape(nx + 1, in_late, HALF, LANES)
    group, from_y, from_x, bnd_all, landed = exchange(
        0, ny, nx, [shard.reshape(-1, LANES)], [to_y, to_x], bnd, parts
    )
    block_rows, col_at = pl.pallas_call(
        functools.partial(build_kernel, ny, nx),
        name="build",
        out_shape=[
            jax.ShapeDtypeStruct((LB, 2 * KB, SLOTS * HALF), BF16),
            jax.ShapeDtypeStruct((LB * SLOTS,), jnp.int32),
        ],
        in_specs=[SMEM] * 5 + [VMEM] * 6,
        out_specs=[VMEM, SMEM],
        scratch_shapes=[pltpu.SMEM((GROUPS * LB,), jnp.int32), pltpu.SMEM((LB,), jnp.int32)],
        compiler_params=pltpu.CompilerParams(vmem_limit_bytes=LIMIT),
    )(in_row, in_col, back_at, if_row, if_src, own_val, to_y, to_x, from_y, from_x, if_val)
    blocks_all = n_row * LB + n_sub * IFR
    image_x, gram = plain(
        first_apply_kernel,
        "first_apply",
        [SMEM] * 2 + [VMEM] * 6,
        [shape(rows_here, LANES), shape(LANES, LANES)],
        [pltpu.VMEM((blocks_all, HALF, 2 * LANES), BF16)],
        col_at,
        bnd_rows,
        block_rows,
        shard,
        group.reshape(n_row, LB, HALF, LANES),
        bnd_all,
        landed,
        current,
    )
    metric, group_p, bnd_p, landed_p = sum_beside_exchange(1, ny, nx, gram, shard_p.reshape(-1, LANES), bnd_p, parts_p)
    basis, packed, bnd, parts = plain(
        first_ritz_kernel,
        "first_ritz",
        [SMEM] * 3 + [VMEM] * 5,
        [shape(rows_here, LANES), *sent(1)],
        [pltpu.VMEM((rows_here, LANES), F32), pltpu.VMEM((KB, LANES), F32)],
        *faces,
        metric,
        if_val,
        weights,
        current,
        image_x,
    )
    metric = metric[:KB]
    solver = [pltpu.VMEM((rows_here, LANES), F32), pltpu.VMEM((LANES, 2 * LANES), F32), pltpu.VMEM((KB, LANES), F32)]
    for sweep in range(ITERS):
        group, bnd_all, landed = exchange(2 + 2 * sweep, ny, nx, [packed.reshape(-1, LANES)], [], bnd, parts)
        coarse = sweep == ITERS - 1
        images = plain(
            functools.partial(apply_kernel, coarse),
            f"apply_{sweep}",
            [SMEM] * 2 + [VMEM] * (11 if sweep == 0 else 7),
            [shape(rows_here, LANES)] * (2 if coarse else 1),
            [pltpu.VMEM((blocks_all, HALF, LANES if coarse else 2 * LANES), BF16)],
            col_at,
            bnd_rows,
            block_rows,
            packed,
            group.reshape(n_row, LB, HALF, LANES),
            bnd_all,
            landed,
            *((shard_p, group_p.reshape(n_row, LB, HALF, LANES), bnd_p, landed_p) if sweep == 0 else ()),
            image_x,
            basis,
        )
        image_b = images[0]
        gram = sum_grams(3 + 2 * sweep, n_sub, n_row, [current, image_x, basis, *images])
        if sweep < ITERS - 1:
            metric, current, image_x, basis, packed, bnd, parts = plain(
                functools.partial(step_kernel, total_rows),
                "step",
                [SMEM] * 3 + [VMEM] * 8,
                [shape(KB, LANES), shape(rows_here, LANES), shape(rows_here, LANES), shape(rows_here, LANES), *sent(1, BF16)],
                solver,
                *faces,
                gram,
                metric,
                if_val,
                weights,
                current,
                image_x,
                basis,
                image_b,
            )
    modes, search = plain(
        functools.partial(last_kernel, total_rows),
        "last",
        [VMEM] * 4,
        [shape(KB, rows_here), shape(KB, rows_here)],
        solver,
        gram,
        metric,
        current,
        basis,
    )
    return modes.T, search.T


def solution(mesh):
    n_sub, n_row = mesh.shape["sub"], mesh.shape["row"]
    ny = 4 if n_row == 16 else 2
    return jax.shard_map(
        functools.partial(local, (n_sub, ny, n_row // ny)),
        mesh=mesh,
        in_specs=(
            P(("sub", "row"), None),
            P(("sub", "row"), None),
            P(("sub", "row")),
            P("sub", "row", None),
            P("sub", "row", None),
            P("sub", "row", None, None, None),
            P("sub", "row", None),
            P("sub", "row", None),
            P("sub", "row", None),
            P("sub", "row", None, None, None),
        ),
        out_specs=(P(("sub", "row"), None), P(("sub", "row"), None)),
        check_vma=False,
    )
```
